32 devices in a mesh: field: 2 (over core), tm: 16 (over z, y, x).
Axes of the slice: x: 2, y: 2, z: 4, core: 2. Of those that a mesh axis runs over, the one named last changes fastest.
Arguments:
- observed: float32 [2, 262144], P('field', 'tm'), may hold values from -6 to 6
- weights: float32 [2, 262144], P('field', 'tm'), may hold values from 0.5 to 4
- features: float32 [2, 8, 262144], P('field', None, 'tm'), may hold values from -4 to 4
- source_ids: int32 [2, 262144], P('field', 'tm'), may hold values from 0 to 8191
- ccd_ids: int32 [2, 262144], P('field', 'tm'), may hold values from 0 to 61
- unit_ids: int32 [2, 262144], P('field', 'tm'), may hold values from 0 to 3
- counts: int32 [2, 512], P('field', 'tm'), may hold values from 256 to 512, as said below
- shared_cal: float32 [64, 4, 62], P('tm'), may hold values from -3 to 3
- field_cal: float32 [2, 64, 4, 62], P('field', 'tm'), may hold values from -3 to 3
Outputs:
- source_mean: float32 [262144], P(('field', 'tm'))
- new_shared: float32 [2, 64, 4, 62], P('field', 'tm')
- new_field: float32 [2, 64, 4, 62], P('field', 'tm')
The draws below stay inside these ranges and needn't reach their ends.
Inputs may be any that keep to these rules, and one draw needn't show every extreme that they name: `counts`: every device sends at most 512 live transits to each owner; one owner receives exactly 512 from every device; live transits fill the first slots of a block.
All inputs are finite; a program needn't handle non-finite values.
Results may differ from the reference program's by a relative error of at most 0.0003.
Values sent between devices are 32-bit elements; how exact they have to be, the bound alone decides.
A program may use at most 64 MiB of HBM per device.

```python
import math
import jax
import jax.numpy as jnp
import numpy as np
from jax import lax

CCD = 62
KS = 4
KF = 4
UNITS_DEV = 4
CAP = 512
SRC_DEV = 8192
K = 8
SLOTS = 16384
UNITS = 64
SOURCES = 262144
N_FIELD = 2
N_TM = 16
DEVICES = 32


def draw_counts(key, part):
    first_key, second_key = jax.random.split(key, 2)
    filled = jax.random.randint(first_key, (DEVICES, DEVICES), CAP - CAP // 2, CAP + 1)
    full_owner = jax.random.randint(second_key, (), 0, DEVICES)
    column = jnp.arange(DEVICES)[None, :] == full_owner
    filled = jnp.where(column, CAP, filled)
    return filled.reshape(N_FIELD, N_TM * DEVICES).astype(jnp.int32)


def plant(values, key, least, top_value):
    shape = values.shape
    index_at = [jax.random.randint(jax.random.fold_in(key, axis), (), 0, shape[axis]) for axis in range(len(shape))]
    values = values.at[tuple(index_at)].set(least)
    longest = shape.index(max(shape))
    index_at[longest] = (index_at[longest] + 1) % shape[longest]
    return values.at[tuple(index_at)].set(top_value)


def block_levels(key, shape, cuts, least, top_value):
    gain, own = 1.0, jax.random.fold_in(key, 6)
    for dim, blocks in cuts:
        heights = jnp.exp(jax.random.uniform(jax.random.fold_in(own, dim), (blocks,), jnp.float32, least / len(cuts), top_value / len(cuts)))
        gain = gain * jnp.repeat(heights, shape[dim] // blocks).reshape([-1 if axis == dim else 1 for axis in range(len(shape))])
    return gain


def rank_table(amount, skew):
    portions = [(1 << 20) // math.isqrt(standing ** skew) + 1 for standing in range(1, amount + 1)]
    spread = 1 + sum(portions) // (1 << 30)
    return np.cumsum(np.array([max(1, weight // spread) for weight in portions]))


def ranked(key, shape, count, slope):
    grid = rank_table(count, slope)
    ticket = jax.random.randint(jax.random.fold_in(key, 1), shape, 0, int(grid[count - 1]))
    standing = jnp.searchsorted(jnp.asarray(grid, jnp.int32), ticket, side="right")
    return jax.random.permutation(jax.random.fold_in(key, 2), count)[standing].astype(jnp.int32)


def gaussian(key, shape, deviation, reach, cuts=(), kind=jnp.bfloat16):
    drawn = jax.random.normal(key, shape, jnp.float32) * deviation
    if len(cuts) > 0:
        drawn = block_levels(key, shape, cuts, -0.22, 0.18) * drawn
    return jnp.clip(drawn, min=-reach, max=reach).astype(kind)


def setup_inputs(seed: int = 0) -> dict:
    seeds = jax.random.split(jax.random.key(seed), 10)
    return {
        "observed": gaussian(seeds[0], (N_FIELD, N_TM * SLOTS), 1.0, 6.0, ((0, 2), (1, 16)), jnp.float32),
        "weights": jnp.clip(jnp.exp(math.log(4.0) - 2.0794415 * jax.random.uniform(seeds[1], (N_FIELD, N_TM * SLOTS), jnp.float32) ** block_levels(seeds[1], (N_FIELD, N_TM * SLOTS), ((0, 2), (1, 16)), -0.2, 0.2)), 0.5, 4.0),
        "features": gaussian(seeds[2], (N_FIELD, K, N_TM * SLOTS), 1.0, 4.0, ((0, 2), (2, 16)), jnp.float32),
        "source_ids": plant(ranked(seeds[3], (N_FIELD, N_TM * SLOTS), SRC_DEV, 2), jax.random.fold_in(seeds[3], 3), 0, SRC_DEV - 1).astype(jnp.int32),
        "ccd_ids": plant(jax.random.randint(seeds[4], (N_FIELD, N_TM * SLOTS), 0, CCD), jax.random.fold_in(seeds[4], 1), 0, CCD - 1).astype(jnp.int32),
        "unit_ids": plant(jax.random.randint(seeds[5], (N_FIELD, N_TM * SLOTS), 0, UNITS_DEV), jax.random.fold_in(seeds[5], 1), 0, UNITS_DEV - 1).astype(jnp.int32),
        "counts": draw_counts(jax.random.fold_in(seeds[9], 71), 0),
        "shared_cal": gaussian(seeds[7], (UNITS, KS, CCD), 0.5, 3.0, ((0, 16),), jnp.float32),
        "field_cal": gaussian(seeds[8], (N_FIELD, UNITS, KF, CCD), 0.5, 3.0, ((0, 2), (1, 16)), jnp.float32),
    }


RIDGE = 1.0


def feature_rows(basis_block, weight_block, resid_block, n_shared, n_field):
    weighted = weight_block[None, :] * basis_block
    products = []
    for i in range(n_shared):
        for j in range(n_shared):
            products.append(weighted[i] * basis_block[j])
    for i in range(n_shared):
        products.append(weighted[i] * resid_block)
    for i in range(n_field):
        for j in range(n_field):
            products.append(weighted[n_shared + i] * basis_block[n_shared + j])
    for i in range(n_field):
        products.append(weighted[n_shared + i] * resid_block)
    return jnp.stack(products)


def solve_small(matrix, vector):
    n = vector.shape[0]
    a = [[matrix[i, j] for j in range(n)] for i in range(n)]
    b = [vector[i] for i in range(n)]
    for p in range(n):
        for i in range(p + 1, n):
            factor = a[i][p] / a[p][p]
            for j in range(p, n):
                a[i][j] = a[i][j] - factor * a[p][j]
            b[i] = b[i] - factor * b[p]
    x = [None] * n
    for i in reversed(range(n)):
        running = b[i]
        for j in range(i + 1, n):
            running = running - a[i][j] * x[j]
        x[i] = running / a[i][i]
    return jnp.stack(x)


def solve_block(normal_sums, k):
    batch = normal_sums.shape[1]
    matrix = normal_sums[: k * k].reshape(k, k, batch) + RIDGE * jnp.eye(k, dtype=jnp.float32)[:, :, None]
    return solve_small(matrix, normal_sums[k * k:])


def reference(observed, weights, features, source_ids, ccd_ids, unit_ids, counts, shared_cal, field_cal):
    device_count = N_FIELD * N_TM
    k_all = KS + KF
    segments = UNITS_DEV * CCD
    n_shared_rows = KS * KS + KS
    obs_dev = observed.reshape(device_count, SLOTS)
    wts_dev = weights.reshape(device_count, SLOTS)
    feat_dev = features.reshape(N_FIELD, k_all, N_TM, SLOTS).transpose(0, 2, 1, 3).reshape(device_count, k_all, SLOTS)
    src_dev = source_ids.reshape(device_count, SLOTS)
    ccd_dev = ccd_ids.reshape(device_count, SLOTS)
    unit_dev = unit_ids.reshape(device_count, SLOTS)
    count_dev = counts.reshape(device_count, DEVICES)
    shared_tab = shared_cal.reshape(N_TM, UNITS_DEV, KS, CCD).transpose(0, 2, 1, 3).reshape(N_TM, KS, segments)
    shared_tab = jnp.broadcast_to(shared_tab[None], (N_FIELD, N_TM, KS, segments)).reshape(device_count, KS, segments)
    field_tab = field_cal.reshape(N_FIELD, N_TM, UNITS_DEV, KF, CCD).transpose(0, 1, 3, 2, 4).reshape(device_count, KF, segments)
    lookup = jnp.concatenate([shared_tab, field_tab], axis=1)

    def section_one(items):
        obs_one, wts_one, feat_one, src_one, ccd_one, unit_one, count_one, lookup_one = items
        position = lax.broadcasted_iota(jnp.int32, (DEVICES, CAP), 1)
        inside = (position < count_one[:, None]).reshape(SLOTS)
        segment = (unit_one * CCD + ccd_one).astype(jnp.int32)
        picked = jnp.take(lookup_one, segment, axis=1)
        correction = jnp.sum(feat_one * picked, axis=0)
        calibrated = obs_one - correction
        weight_used = jnp.where(inside, wts_one, jnp.zeros_like(wts_one))
        owner_ids = jnp.where(inside, src_one, 0).astype(jnp.int32)
        return calibrated, weight_used, owner_ids, segment

    calibrated, weight_used, owner_ids, segment = lax.map(
        section_one, (obs_dev, wts_dev, feat_dev, src_dev, ccd_dev, unit_dev, count_dev, lookup))
    owner = (jnp.arange(SLOTS, dtype=jnp.int32) // CAP).astype(jnp.int32)
    global_ids = (owner[None, :] * SRC_DEV + owner_ids).astype(jnp.int32).reshape(-1)
    totals = jax.ops.segment_sum((weight_used * calibrated).reshape(-1), global_ids, num_segments=SOURCES)
    weight_sum = jax.ops.segment_sum(weight_used.reshape(-1), global_ids, num_segments=SOURCES)
    source_mean = totals / (weight_sum + 1.0)
    residual = calibrated - jnp.take(source_mean, global_ids).reshape(device_count, SLOTS)

    def section_two(items):
        feat_one, weight_one, resid_one, segment_one = items
        products = feature_rows(feat_one, weight_one, resid_one, KS, KF)
        return jax.ops.segment_sum(products.T, segment_one, num_segments=segments).T

    normal_sums = lax.map(section_two, (feat_dev, weight_used, residual, segment))
    normal_sums = normal_sums.reshape(N_FIELD, N_TM, normal_sums.shape[1], segments)
    shared_total = normal_sums[0, :, :n_shared_rows] + normal_sums[1, :, :n_shared_rows]
    shared_total = shared_total.transpose(1, 0, 2).reshape(n_shared_rows, N_TM * segments)
    delta_shared = solve_block(shared_total, KS)
    delta_shared = delta_shared.reshape(KS, N_TM, UNITS_DEV, CCD).transpose(1, 2, 0, 3).reshape(UNITS, KS, CCD)
    field_sums = normal_sums[:, :, n_shared_rows:]
    n_field_rows = field_sums.shape[2]
    field_sums = field_sums.transpose(2, 0, 1, 3).reshape(n_field_rows, device_count * segments)
    delta_field = solve_block(field_sums, KF)
    delta_field = delta_field.reshape(KF, N_FIELD, N_TM, UNITS_DEV, CCD).transpose(1, 2, 3, 0, 4).reshape(N_FIELD, UNITS, KF, CCD)
    new_shared = jnp.broadcast_to((shared_cal + delta_shared)[None], (N_FIELD, UNITS, KS, CCD))
    return source_mean, new_shared, field_cal + delta_field
```

```python
import functools

import jax
import jax.numpy as jnp
from jax import lax
from jax.experimental import pallas as pl
from jax.experimental.pallas import tpu as pltpu
from jax.sharding import PartitionSpec as P

SRC_DEV = 8192
RIDGE = 1.0
UNROLL = 8
LANES = 128
SUB = 8
F32 = jnp.float32
BF16 = jnp.bfloat16
CCD_PAD = 64


def split_pair(x):
    high = x.astype(BF16).astype(F32)
    return jnp.concatenate([x, x - high], axis=0).astype(BF16)


def row_of(x, j, rows):
    return jnp.broadcast_to(x[j : j + 1, :], (rows, x.shape[1]))


def bf16_rows(count):
    return lax.broadcasted_iota(jnp.int32, (count, LANES), 0).astype(F32).astype(BF16)


def wide_row(row, count):
    one = jnp.broadcast_to(row.astype(F32), (2 * SUB, LANES)).astype(BF16)
    return jnp.concatenate([one] * (count // (2 * SUB)), axis=0)


def hot_rows(index_row, rows):
    hit = rows == wide_row(index_row, rows.shape[0])
    return jnp.where(hit, jnp.ones_like(rows), jnp.zeros_like(rows))


def pick(table, index):
    return jnp.take_along_axis(table, index, axis=1, mode="promise_in_bounds")


def nt_dot(left, right):
    return lax.dot_general(
        left, right, (((1,), (1,)), ((), ())), preferred_element_type=F32
    )


def build_tables(shared_ref, field_ref, tab_ref):
    units, n_shared, ccds = shared_ref.shape
    tab_ref[...] = jnp.zeros_like(tab_ref)
    for u in range(units):
        tab_ref[u, 0:n_shared, 0:ccds] = shared_ref[u]
        tab_ref[u, n_shared : 2 * n_shared, 0:ccds] = field_ref[u]


def used_weights(g, wts, cnt_ref, rows_per_block):
    sub = lax.broadcasted_iota(jnp.int32, (SUB, LANES), 0)
    lane = lax.broadcasted_iota(jnp.int32, (SUB, LANES), 1)
    position = (sub % rows_per_block) * LANES + lane
    per_group = SUB // rows_per_block
    limit = jnp.full((SUB, LANES), cnt_ref[0, g * per_group], jnp.int32)
    for b in range(1, per_group):
        limit = jnp.where(sub >= b * rows_per_block, cnt_ref[0, g * per_group + b], limit)
    return jnp.where(position < limit, wts, 0.0)


def feat_rows(feat_ref, row):
    return feat_ref[:, pl.ds(pl.multiple_of(row * LANES, LANES), LANES)]


def calibrate_rows(g, obs, ccd, unit, feat_ref, tables):
    index = ccd + (unit & 1) * CCD_PAD
    corrections = []
    for j in range(SUB):
        index_b = row_of(index, j, SUB)
        unit_b = row_of(unit, j, SUB)
        picked = jnp.where(unit_b < 2, pick(tables[0], index_b), pick(tables[1], index_b))
        corrections.append(jnp.sum(feat_rows(feat_ref, g * SUB + j) * picked, axis=0, keepdims=True))
    return obs - jnp.concatenate(corrections, axis=0)


def masked_units(pairs, unit_row, units):
    unit_b = jnp.broadcast_to(unit_row.astype(F32), (2 * SUB, LANES)).astype(BF16)
    zero = jnp.zeros((2 * SUB, LANES), BF16)
    out = []
    for u in range(units):
        own = unit_b == jnp.asarray(u, BF16)
        out += [jnp.where(own, pair, zero) for pair in pairs]
    return jnp.concatenate(out, axis=0)


def matrix_rows(g, weight_used, ccd, unit, feat_ref, units, ccd_rows):
    sub = lax.broadcasted_iota(jnp.int32, (SUB, LANES), 0) % 4
    left, hot = [], []
    for j in range(SUB):
        feats = feat_rows(feat_ref, g * SUB + j)
        weighted = row_of(weight_used, j, SUB) * feats
        next_one = jnp.where(sub == 3, pltpu.roll(feats, 3, 0), pltpu.roll(feats, 7, 0))
        next_two = jnp.where(sub >= 2, pltpu.roll(feats, 2, 0), pltpu.roll(feats, 6, 0))
        pairs = [split_pair(weighted * other) for other in (feats, next_one, next_two)]
        left.append(masked_units(pairs, unit[j : j + 1, :], units))
        hot.append(hot_rows(ccd[j : j + 1, :], ccd_rows))
    return nt_dot(jnp.concatenate(left, axis=1), jnp.concatenate(hot, axis=1))


def vector_rows(g, scaled, ccd, unit, feat_ref, units, ccd_rows):
    left, hot = [], []
    for j in range(SUB):
        feats = feat_rows(feat_ref, g * SUB + j)
        left.append(masked_units([split_pair(row_of(scaled, j, SUB) * feats)], unit[j : j + 1, :], units))
        hot.append(hot_rows(ccd[j : j + 1, :], ccd_rows))
    return nt_dot(jnp.concatenate(left, axis=1), jnp.concatenate(hot, axis=1))


def source_rows(values, ids, high_rows, low_rows):
    high, low = ids >> 7, ids & (LANES - 1)
    top = values.astype(BF16).astype(F32)
    rest = values - top
    zero = jnp.zeros_like(high_rows)
    count = high_rows.shape[0]
    left, hot = [], []
    for j in range(SUB):
        hot.append(hot_rows(low[j : j + 1, :], low_rows))
        hit = high_rows == wide_row(high[j : j + 1, :], count)
        left.append(jnp.concatenate(
            [jnp.where(hit, wide_row(x[j : j + 1, :], count), zero) for x in (top, rest)], axis=0))
    return nt_dot(jnp.concatenate(left, axis=1), jnp.concatenate(hot, axis=1))


def read_rows(mean_ref, ids):
    high, low = ids >> 7, ids & (LANES - 1)
    out = jnp.zeros((SUB, LANES), F32)
    for h in range(SRC_DEV // LANES):
        row = jnp.broadcast_to(mean_ref[h : h + 1, :], (SUB, LANES))
        out = jnp.where(high == h, pick(row, low), out)
    return out


def solve_rows(matrix, vector):
    n = len(vector)
    a = [[None] * n for _ in range(n)]
    for i in range(n):
        a[i][i] = matrix[0][i] + RIDGE
        k = (i + 1) % n
        a[i][k] = a[k][i] = matrix[1][i]
    for i in range(n // 2):
        a[i][i + 2] = a[i + 2][i] = matrix[2][i]
    b = list(vector)
    for p in range(n):
        for i in range(p + 1, n):
            factor = a[i][p] / a[p][p]
            for j in range(p, n):
                a[i][j] = a[i][j] - factor * a[p][j]
            b[i] = b[i] - factor * b[p]
    x = [None] * n
    for i in reversed(range(n)):
        running = b[i]
        for j in range(i + 1, n):
            running = running - a[i][j] * x[j]
        x[i] = running / a[i][i]
    return x


def whole_kernel(
    n_tm, rows_per_block,
    obs_h, wts_h, src_h, ccd_h, unit_h, feat_h, cnt_h, shared_h, field_h,
    mean_ref, new_shared_ref, new_field_ref,
    obs_ref, wts_ref, src_ref, ccd_ref, unit_ref, feat_ref, cnt_ref, shared_ref, field_ref,
    tab_ref, wu_ref, cal_ref, pack, pack_in, vals, vals_in, ans, ans_in,
    mat_ref, vec_ref, val_sum, wt_sum, mx, mx_in, vx, vx_in,
    load_sem, send_sem, recv_sem,
):
    units, n, ccds = shared_ref.shape
    devices = pack.shape[0]
    groups = obs_ref.shape[0] // SUB
    field, tm = lax.axis_index("field"), lax.axis_index("tm")
    me = field * n_tm + tm
    my_group = me // (SUB // rows_per_block)

    loads = [
        pltpu.make_async_copy(a, b, load_sem.at[i])
        for i, (a, b) in enumerate((
            (wts_h, wts_ref), (src_h, src_ref), (cnt_h, cnt_ref), (shared_h, shared_ref), (field_h, field_ref),
            (obs_h, obs_ref), (ccd_h, ccd_ref), (unit_h, unit_ref), (feat_h, feat_ref)))
    ]
    for load in loads:
        load.start()

    def wrap(x, size):
        return jnp.where(x >= size, x - size, x)

    def place(e):
        return jnp.where(e >= n_tm, 1, 0), wrap(e, n_tm)

    def target(k):
        e = wrap(me + k, devices)
        return e, place(e)

    barrier = pltpu.get_barrier_semaphore()

    def greet(k, carry):
        pl.semaphore_signal(barrier, inc=1, device_id=target(k)[1], device_id_type=pl.DeviceIdType.MESH)
        return carry

    for k in range(1, devices):
        greet(k, 0)

    def send(phase, source, landing, e):
        pltpu.make_async_remote_copy(
            src_ref=source.at[e], dst_ref=landing.at[me], send_sem=send_sem.at[phase], recv_sem=recv_sem.at[phase],
            device_id=place(e), device_id_type=pl.DeviceIdType.MESH).start()

    def await_bytes(ref, sem):
        part = ref.at[pl.ds(0, devices - 1)]
        pltpu.make_async_copy(part, part, sem).wait()

    def rows_at(g):
        return pl.ds(pl.multiple_of(g * SUB, SUB), SUB)

    def pair(ref, g):
        per = SUB // rows_per_block
        return jnp.concatenate([ref[g * per + b, 0:rows_per_block, :] for b in range(per)], axis=0)

    def weights_in(g):
        per = SUB // rows_per_block
        return jnp.concatenate([pack_in[g * per + b, rows_per_block:, :] for b in range(per)], axis=0)

    def ids_in(g):
        return pair(pack_in, g).astype(jnp.int32)

    def put(ref, g, x, first=0):
        per = SUB // rows_per_block
        for b in range(per):
            ref[g * per + b, first : first + rows_per_block, :] = x[b * rows_per_block : (b + 1) * rows_per_block]

    def turn(step):
        return wrap(my_group + step, groups)

    def in_halves(body, phase, source, landing):
        per = SUB // rows_per_block
        base = my_group * per
        half = groups // 2
        for part in range(2):
            lax.fori_loop(part * half, (part + 1) * half, body, 0, unroll=UNROLL)
            if part == 0:
                for i in range(1, per):
                    send(phase, source, landing, base + lax.rem(me - base + i, per))
            for k in range(part * half * per + (per if part == 0 else 0), (part + 1) * half * per):
                send(phase, source, landing, wrap(base + k, devices))

    for load in loads[:3]:
        load.wait()

    def prepare(g, carry):
        wu = used_weights(g, wts_ref[rows_at(g), :], cnt_ref, rows_per_block)
        wu_ref[rows_at(g), :] = wu
        put(pack, g, src_ref[rows_at(g), :].astype(F32))
        put(pack, g, wu, rows_per_block)
        return carry

    lax.fori_loop(0, groups, prepare, 0, unroll=UNROLL)
    pack_in[me] = pack[me]
    pl.semaphore_wait(barrier, devices - 1)

    def send_pack(k, carry):
        send(0, pack, pack_in, target(k)[0])
        return carry

    for k in range(1, devices):
        send_pack(k, 0)

    for load in loads[3:]:
        load.wait()
    build_tables(shared_ref, field_ref, tab_ref)
    tables = [tab_ref[2 * t] + pltpu.roll(tab_ref[2 * t + 1], CCD_PAD, 1) for t in range(units // 2)]

    def calibrate(step, carry):
        g = turn(step)
        at = rows_at(g)
        cal = calibrate_rows(g, obs_ref[at, :], ccd_ref[at, :], unit_ref[at, :], feat_ref, tables)
        cal_ref[at, :] = cal
        put(vals, g, wu_ref[at, :] * cal)
        return carry

    in_halves(calibrate, 1, vals, vals_in)
    vals_in[me] = vals[me]

    ccd_rows, low_rows = bf16_rows(CCD_PAD), bf16_rows(LANES)
    high_rows = bf16_rows(SRC_DEV // LANES)
    mat_ref[...] = jnp.zeros_like(mat_ref)
    vec_ref[...] = jnp.zeros_like(vec_ref)
    val_sum[...] = jnp.zeros_like(val_sum)
    wt_sum[...] = jnp.zeros_like(wt_sum)

    def add_matrix(g, carry):
        at = rows_at(g)
        mat_ref[...] += matrix_rows(g, wu_ref[at, :], ccd_ref[at, :], unit_ref[at, :], feat_ref, units, ccd_rows)
        return carry

    lax.fori_loop(0, groups, add_matrix, 0, unroll=UNROLL)

    def entry(ref, pieces, piece, row):
        out = []
        for u in range(units):
            base = (u * pieces + piece) * 2 * SUB + row
            out.append(ref[base : base + 1, :] + ref[base + SUB : base + SUB + 1, :])
        return jnp.concatenate(out, axis=0)

    def partner_copy(source, landing, phase):
        return pltpu.make_async_remote_copy(
            src_ref=source, dst_ref=landing, send_sem=send_sem.at[phase], recv_sem=recv_sem.at[phase],
            device_id=(1 - field, tm), device_id_type=pl.DeviceIdType.MESH)

    for d in range(3):
        for i in range(n):
            mx[d * n + i] = entry(mat_ref, 3, d, i)
    matrix_copy = partner_copy(mx, mx_in, 3)
    matrix_copy.start()

    await_bytes(pack_in, recv_sem.at[0])

    def add_weights(g, carry):
        wt_sum[...] += source_rows(weights_in(g), ids_in(g), high_rows, low_rows)
        return carry

    lax.fori_loop(0, groups, add_weights, 0, unroll=UNROLL)
    await_bytes(vals_in, recv_sem.at[1])

    def add_values(g, carry):
        val_sum[...] += source_rows(pair(vals_in, g), ids_in(g), high_rows, low_rows)
        return carry

    lax.fori_loop(0, groups, add_values, 0, unroll=UNROLL)
    count = SRC_DEV // LANES
    mean_ref[...] = (val_sum[:count] + val_sum[count:]) / ((wt_sum[:count] + wt_sum[count:]) + 1.0)

    def answer(step, carry):
        g = turn(step)
        put(ans, g, read_rows(mean_ref, ids_in(g)))
        return carry

    in_halves(answer, 2, ans, ans_in)
    ans_in[me] = ans[me]
    await_bytes(ans_in, recv_sem.at[2])

    def add_vector(g, carry):
        at = rows_at(g)
        scaled = wu_ref[at, :] * (cal_ref[at, :] - pair(ans_in, g))
        vec_ref[...] += vector_rows(g, scaled, ccd_ref[at, :], unit_ref[at, :], feat_ref, units, ccd_rows)
        return carry

    lax.fori_loop(0, groups, add_vector, 0, unroll=UNROLL)
    for i in range(n):
        vx[i] = entry(vec_ref, 1, 0, i)
    vector_copy = partner_copy(vx, vx_in, 4)
    vector_copy.start()

    def finish(matrix, vector, old_ref, new_ref):
        for i, x in enumerate(solve_rows(matrix, vector)):
            for u in range(units):
                new_ref[u, i : i + 1, :] = old_ref[u, i : i + 1, :] + x[u : u + 1, :ccds]

    finish([[entry(mat_ref, 3, d, n + i) for i in range(n)] for d in range(3)],
           [entry(vec_ref, 1, 0, n + i) for i in range(n)], field_ref, new_field_ref)
    matrix_copy.wait()
    vector_copy.wait()
    finish([[mx[d * n + i] + mx_in[d * n + i] for i in range(n)] for d in range(3)],
           [vx[i] + vx_in[i] for i in range(n)], shared_ref, new_shared_ref)
    await_bytes(pack, send_sem.at[0])
    await_bytes(vals, send_sem.at[1])
    await_bytes(ans, send_sem.at[2])


def hand_on(*refs):
    copies = [pltpu.make_async_copy(refs[i], refs[3 + i], refs[6].at[i]) for i in range(3)]
    for copy in copies:
        copy.start()
    for copy in copies:
        copy.wait()


def per_device(n_tm, observed, weights, features, source_ids, ccd_ids, unit_ids, counts, shared_cal, field_cal):
    slots = observed.shape[1]
    devices = counts.shape[1]
    rows = slots // LANES
    block = rows // devices
    units, n, ccds = shared_cal.shape
    obs, wts, src, ccd, unit = (
        x.reshape(rows, LANES) for x in (observed, weights, source_ids, ccd_ids, unit_ids))
    high = SRC_DEV // LANES
    vm = lambda *shape: pltpu.VMEM(shape, F32)
    vi = lambda *shape: pltpu.VMEM(shape, jnp.int32)
    blocks = vm(devices, block, LANES)
    mean, new_shared, new_field = pl.pallas_call(
        functools.partial(whole_kernel, n_tm, block),
        out_shape=[pltpu.VMEM((high, LANES), F32), pltpu.VMEM((units, n, ccds), F32), pltpu.VMEM((units, n, ccds), F32)],
        in_specs=[pl.BlockSpec(memory_space=pl.ANY)] * 9,
        out_specs=[pl.BlockSpec(memory_space=pltpu.VMEM)] * 3,
        scratch_shapes=[
            vm(rows, LANES), vm(rows, LANES), vi(rows, LANES), vi(rows, LANES), vi(rows, LANES),
            vm(2 * n, slots), pltpu.SMEM((1, devices), jnp.int32), vm(units, n, ccds), vm(units, n, ccds),
            vm(units, 2 * n, LANES), vm(rows, LANES), vm(rows, LANES),
            vm(devices, 2 * block, LANES), vm(devices, 2 * block, LANES), blocks, blocks, blocks, blocks,
            vm(units * 3 * 2 * SUB, CCD_PAD), vm(units * 2 * SUB, CCD_PAD), vm(2 * high, LANES), vm(2 * high, LANES),
            vm(3 * n, units, CCD_PAD), vm(3 * n, units, CCD_PAD), vm(n, units, CCD_PAD), vm(n, units, CCD_PAD),
            pltpu.SemaphoreType.DMA((9,)), pltpu.SemaphoreType.DMA((5,)), pltpu.SemaphoreType.DMA((5,)),
        ],
        compiler_params=pltpu.CompilerParams(
            collective_id=0, has_side_effects=True, vmem_limit_bytes=56 * 1024 * 1024),
    )(obs, wts, src, ccd, unit, features[0], counts, shared_cal, field_cal[0])
    mean, new_shared, new_field = pl.pallas_call(
        hand_on,
        out_shape=[jax.ShapeDtypeStruct(x.shape, F32) for x in (mean, new_shared, new_field)],
        in_specs=[pl.BlockSpec(memory_space=pl.ANY)] * 3,
        out_specs=[pl.BlockSpec(memory_space=pl.ANY)] * 3,
        scratch_shapes=[pltpu.SemaphoreType.DMA((3,))],
    )(*(pltpu.with_memory_space_constraint(x, pltpu.VMEM) for x in (mean, new_shared, new_field)))
    return mean.reshape(SRC_DEV), new_shared[None], new_field[None]


def solution(mesh):
    in_specs = (
        P("field", "tm"),
        P("field", "tm"),
        P("field", None, "tm"),
        P("field", "tm"),
        P("field", "tm"),
        P("field", "tm"),
        P("field", "tm"),
        P("tm", None, None),
        P("field", "tm", None, None),
    )
    out_specs = (P(("field", "tm")), P("field", "tm", None, None), P("field", "tm", None, None))
    return jax.shard_map(
        functools.partial(per_device, mesh.shape["tm"]), mesh=mesh, in_specs=in_specs, out_specs=out_specs, check_vma=False
    )
```

```python
import functools

import jax
import jax.numpy as jnp
from jax import lax
from jax.experimental import pallas as pl
from jax.experimental.pallas import tpu as pltpu
from jax.sharding import PartitionSpec as P

SRC_DEV = 8192
RIDGE = 1.0
UNROLL = 8
CHUNK = 4
CHUNK_UNROLL = 4
LANES = 128
SUB = 8
F32 = jnp.float32
BF16 = jnp.bfloat16
CCD_PAD = 64


def split_pair(x):
    high = x.astype(BF16).astype(F32)
    return jnp.concatenate([x, x - high], axis=0).astype(BF16)


def row_of(x, j, rows):
    return jnp.broadcast_to(x[j : j + 1, :], (rows, x.shape[1]))


def bf16_rows(count):
    return lax.broadcasted_iota(jnp.int32, (count, LANES), 0).astype(F32).astype(BF16)


def wide_row(row, count):
    one = jnp.broadcast_to(row.astype(F32), (2 * SUB, LANES)).astype(BF16)
    return jnp.concatenate([one] * (count // (2 * SUB)), axis=0)


def hot_rows(index_row, rows):
    hit = rows == wide_row(index_row, rows.shape[0])
    return jnp.where(hit, jnp.ones_like(rows), jnp.zeros_like(rows))


def pick(table, index):
    return jnp.take_along_axis(table, index, axis=1, mode="promise_in_bounds")


def nt_dot(left, right):
    return lax.dot_general(
        left, right, (((1,), (1,)), ((), ())), preferred_element_type=F32
    )


def build_tables(shared_ref, field_ref, tab_ref):
    units, n_shared, ccds = shared_ref.shape
    tab_ref[...] = jnp.zeros_like(tab_ref)
    for u in range(units):
        tab_ref[u, 0:n_shared, 0:ccds] = shared_ref[u]
        tab_ref[u, n_shared : 2 * n_shared, 0:ccds] = field_ref[u]


def used_weights(g, wts, cnt_ref, rows_per_block):
    sub = lax.broadcasted_iota(jnp.int32, (SUB, LANES), 0)
    lane = lax.broadcasted_iota(jnp.int32, (SUB, LANES), 1)
    position = (sub % rows_per_block) * LANES + lane
    per_group = SUB // rows_per_block
    limit = jnp.full((SUB, LANES), cnt_ref[0, g * per_group], jnp.int32)
    for b in range(1, per_group):
        limit = jnp.where(sub >= b * rows_per_block, cnt_ref[0, g * per_group + b], limit)
    return jnp.where(position < limit, wts, 0.0)


def feat_rows(feat_ref, row):
    return feat_ref[:, pl.ds(pl.multiple_of(row * LANES, LANES), LANES)]


def calibrate_rows(g, obs, ccd, unit, feat_ref, tables):
    index = ccd + (unit & 1) * CCD_PAD
    corrections = []
    for j in range(SUB):
        index_b = row_of(index, j, SUB)
        unit_b = row_of(unit, j, SUB)
        picked = jnp.where(unit_b < 2, pick(tables[0], index_b), pick(tables[1], index_b))
        corrections.append(jnp.sum(feat_rows(feat_ref, g * SUB + j) * picked, axis=0, keepdims=True))
    return obs - jnp.concatenate(corrections, axis=0)


def masked_units(pairs, unit_row, units):
    unit_b = jnp.broadcast_to(unit_row.astype(F32), (2 * SUB, LANES)).astype(BF16)
    zero = jnp.zeros((2 * SUB, LANES), BF16)
    out = []
    for u in range(units):
        own = unit_b == jnp.asarray(u, BF16)
        out += [jnp.where(own, pair, zero) for pair in pairs]
    return jnp.concatenate(out, axis=0)


def matrix_rows(g, weight_used, ccd, unit, feat_ref, units, ccd_rows):
    sub = lax.broadcasted_iota(jnp.int32, (SUB, LANES), 0) % 4
    left, hot = [], []
    for j in range(SUB):
        feats = feat_rows(feat_ref, g * SUB + j)
        weighted = row_of(weight_used, j, SUB) * feats
        next_one = jnp.where(sub == 3, pltpu.roll(feats, 3, 0), pltpu.roll(feats, 7, 0))
        next_two = jnp.where(sub >= 2, pltpu.roll(feats, 2, 0), pltpu.roll(feats, 6, 0))
        pairs = [split_pair(weighted * other) for other in (feats, next_one, next_two)]
        left.append(masked_units(pairs, unit[j : j + 1, :], units))
        hot.append(hot_rows(ccd[j : j + 1, :], ccd_rows))
    return nt_dot(jnp.concatenate(left, axis=1), jnp.concatenate(hot, axis=1))


def vector_rows(g, scaled, ccd, unit, feat_ref, units, ccd_rows):
    left, hot = [], []
    for j in range(SUB):
        feats = feat_rows(feat_ref, g * SUB + j)
        left.append(masked_units([split_pair(row_of(scaled, j, SUB) * feats)], unit[j : j + 1, :], units))
        hot.append(hot_rows(ccd[j : j + 1, :], ccd_rows))
    return nt_dot(jnp.concatenate(left, axis=1), jnp.concatenate(hot, axis=1))


def source_rows(ids, weights, values, high_rows, low_rows):
    high, low = ids >> 7, ids & (LANES - 1)
    pieces = []
    for x in (weights, values):
        top = x.astype(BF16).astype(F32)
        pieces += [top, x - top]
    zero = jnp.zeros_like(high_rows)
    count = high_rows.shape[0]
    left, hot = [], []
    for j in range(SUB):
        hot.append(hot_rows(low[j : j + 1, :], low_rows))
        hit = high_rows == wide_row(high[j : j + 1, :], count)
        left.append(jnp.concatenate(
            [jnp.where(hit, wide_row(x[j : j + 1, :], count), zero) for x in pieces], axis=0))
    return nt_dot(jnp.concatenate(left, axis=1), jnp.concatenate(hot, axis=1))


def read_rows(mean_ref, ids):
    high, low = ids >> 7, ids & (LANES - 1)
    out = jnp.zeros((SUB, LANES), F32)
    for h in range(SRC_DEV // LANES):
        row = jnp.broadcast_to(mean_ref[h : h + 1, :], (SUB, LANES))
        out = jnp.where(high == h, pick(row, low), out)
    return out


def solve_rows(matrix, vector):
    n = len(vector)
    a = [[None] * n for _ in range(n)]
    for i in range(n):
        a[i][i] = matrix[0][i] + RIDGE
        k = (i + 1) % n
        a[i][k] = a[k][i] = matrix[1][i]
    for i in range(n // 2):
        a[i][i + 2] = a[i + 2][i] = matrix[2][i]
    b = list(vector)
    for p in range(n):
        for i in range(p + 1, n):
            factor = a[i][p] / a[p][p]
            for j in range(p, n):
                a[i][j] = a[i][j] - factor * a[p][j]
            b[i] = b[i] - factor * b[p]
    x = [None] * n
    for i in reversed(range(n)):
        running = b[i]
        for j in range(i + 1, n):
            running = running - a[i][j] * x[j]
        x[i] = running / a[i][i]
    return x


def whole_kernel(
    n_tm, rows_per_block,
    obs_h, wts_h, src_h, ccd_h, unit_h, feat_h, cnt_h, shared_h, field_h,
    mean_ref, new_shared_ref, new_field_ref,
    obs_ref, wts_ref, src_ref, ccd_ref, unit_ref, feat_ref, cnt_ref, shared_ref, field_ref,
    tab_ref, wu_ref, cal_ref, pack, pack_in, ans, ans_in,
    mat_ref, vec_ref, sum_ref, mx, mx_in, vx, vx_in,
    load_sem, send_sem, recv_sem, chunk_sem,
):
    units, n, ccds = shared_ref.shape
    devices = pack.shape[0]
    groups = obs_ref.shape[0] // SUB
    per = SUB // rows_per_block
    chunk = CHUNK * per
    chunks = devices // chunk
    ring = chunks // 2
    field, tm = lax.axis_index("field"), lax.axis_index("tm")
    me = field * n_tm + tm
    my_chunk = me // chunk
    my_part = my_chunk % ring

    def wrap(x, size):
        return jnp.where(x >= size, x - size, x)

    def place(e):
        return jnp.where(e >= n_tm, 1, 0), wrap(e, n_tm)

    barrier = pltpu.get_barrier_semaphore()
    for k in range(1, devices):
        pl.semaphore_signal(
            barrier, inc=1, device_id=place(wrap(me + k, devices)), device_id_type=pl.DeviceIdType.MESH)

    loads = [
        pltpu.make_async_copy(a, b, load_sem.at[i])
        for i, (a, b) in enumerate((
            (wts_h, wts_ref), (src_h, src_ref), (cnt_h, cnt_ref), (shared_h, shared_ref), (field_h, field_ref),
            (obs_h, obs_ref), (ccd_h, ccd_ref), (unit_h, unit_ref), (feat_h, feat_ref)))
    ]
    for load in loads:
        load.start()

    def chunk_near(step):
        turn, other = step // 2, step % 2
        ahead = jnp.where(turn % 2 == 1, (turn + 1) // 2, wrap(ring - turn // 2, ring))
        return wrap(field + other, 2) * ring + wrap(my_part + ahead, ring)

    def send_chunk(phase, source, landing, c, first=0):
        for i in range(first, chunk):
            e = c * chunk + (me + i) % chunk
            pltpu.make_async_remote_copy(
                src_ref=source.at[e], dst_ref=landing.at[me], send_sem=send_sem.at[phase],
                recv_sem=chunk_sem.at[phase, my_chunk], device_id=place(e), device_id_type=pl.DeviceIdType.MESH).start()
        if first:
            pltpu.make_async_copy(source.at[me], landing.at[me], chunk_sem.at[phase, my_chunk]).start()

    def await_chunk(phase, landing, c):
        part = landing.at[pl.ds(c * chunk, chunk)]
        pltpu.make_async_copy(part, part, chunk_sem.at[phase, c]).wait()

    def await_sent(ref, sem):
        part = ref.at[pl.ds(0, devices - 1)]
        pltpu.make_async_copy(part, part, sem).wait()

    def rows_at(g):
        return pl.ds(pl.multiple_of(g * SUB, SUB), SUB)

    def pair(ref, g, k):
        return jnp.concatenate([ref[g * per + b, k] for b in range(per)], axis=0)

    def ids_in(g):
        return pair(pack_in, g, 0).astype(jnp.int32)

    def put(ref, g, k, x):
        for b in range(per):
            ref[g * per + b, k] = x[b * rows_per_block : (b + 1) * rows_per_block]

    for load in loads:
        load.wait()
    build_tables(shared_ref, field_ref, tab_ref)
    tables = [tab_ref[2 * t] + pltpu.roll(tab_ref[2 * t + 1], CCD_PAD, 1) for t in range(units // 2)]

    def calibrate(g, carry):
        at = rows_at(g)
        wu = used_weights(g, wts_ref[at, :], cnt_ref, rows_per_block)
        cal = calibrate_rows(g, obs_ref[at, :], ccd_ref[at, :], unit_ref[at, :], feat_ref, tables)
        wu_ref[at, :] = wu
        cal_ref[at, :] = cal
        put(pack, g, 0, src_ref[at, :].astype(F32))
        put(pack, g, 1, wu)
        put(pack, g, 2, wu * cal)
        return carry

    lax.fori_loop(0, groups, calibrate, 0, unroll=UNROLL)
    pl.semaphore_wait(barrier, devices - 1)

    def send_pack(step, carry):
        send_chunk(0, pack, pack_in, chunk_near(1 + step))
        return carry

    send_chunk(0, pack, pack_in, my_chunk, 1)
    lax.fori_loop(0, chunks - 1, send_pack, 0, unroll=CHUNK_UNROLL - 1)

    ccd_rows, low_rows = bf16_rows(CCD_PAD), bf16_rows(LANES)
    high_rows = bf16_rows(SRC_DEV // LANES)
    mat_ref[...] = jnp.zeros_like(mat_ref)
    vec_ref[...] = jnp.zeros_like(vec_ref)
    sum_ref[...] = jnp.zeros_like(sum_ref)

    def add_matrix(g, carry):
        at = rows_at(g)
        mat_ref[...] += matrix_rows(g, wu_ref[at, :], ccd_ref[at, :], unit_ref[at, :], feat_ref, units, ccd_rows)
        return carry

    lax.fori_loop(0, groups, add_matrix, 0, unroll=UNROLL)

    def entry(ref, pieces, piece, row):
        out = []
        for u in range(units):
            base = (u * pieces + piece) * 2 * SUB + row
            out.append(ref[base : base + 1, :] + ref[base + SUB : base + SUB + 1, :])
        return jnp.concatenate(out, axis=0)

    def partner_copy(source, landing, phase):
        return pltpu.make_async_remote_copy(
            src_ref=source, dst_ref=landing, send_sem=send_sem.at[2 + phase], recv_sem=recv_sem.at[phase],
            device_id=(1 - field, tm), device_id_type=pl.DeviceIdType.MESH)

    for d in range(3):
        for i in range(n):
            mx[d * n + i] = entry(mat_ref, 3, d, i)
    matrix_copy = partner_copy(mx, mx_in, 0)
    matrix_copy.start()

    def add_sources(step, carry):
        both = [chunk_near(2 * step + k) for k in range(2)]
        for c in both:
            await_chunk(0, pack_in, c)
        total = [sum_ref[k] for k in range(2)]
        for b in range(2 * CHUNK):
            g = both[b // CHUNK] * CHUNK + b % CHUNK
            total[b % 2] += source_rows(ids_in(g), pair(pack_in, g, 1), pair(pack_in, g, 2), high_rows, low_rows)
        for k in range(2):
            sum_ref[k] = total[k]
        return carry

    lax.fori_loop(0, ring, add_sources, 0, unroll=2)
    count = SRC_DEV // LANES
    sums = sum_ref[0] + sum_ref[1]
    mean_ref[...] = (sums[2 * count : 3 * count] + sums[3 * count :]) / ((sums[:count] + sums[count : 2 * count]) + 1.0)

    def answer_chunk(c):
        for b in range(CHUNK):
            g = c * CHUNK + b
            put(ans, g, 0, read_rows(mean_ref, ids_in(g)))

    def answer(step, carry):
        c = chunk_near(chunks - 1 - step)
        answer_chunk(c)
        send_chunk(1, ans, ans_in, c)
        return carry

    lax.fori_loop(0, chunks - 1, answer, 0, unroll=CHUNK_UNROLL - 1)
    answer_chunk(my_chunk)
    send_chunk(1, ans, ans_in, my_chunk, 1)

    def add_vector(step, carry):
        both = [chunk_near(2 * step + k) for k in range(2)]
        for c in both:
            await_chunk(1, ans_in, c)
        total = [vec_ref[k] for k in range(2)]
        for b in range(2 * CHUNK):
            g = both[b // CHUNK] * CHUNK + b % CHUNK
            at = rows_at(g)
            scaled = wu_ref[at, :] * (cal_ref[at, :] - pair(ans_in, g, 0))
            total[b % 2] += vector_rows(g, scaled, ccd_ref[at, :], unit_ref[at, :], feat_ref, units, ccd_rows)
        for k in range(2):
            vec_ref[k] = total[k]
        return carry

    lax.fori_loop(0, ring, add_vector, 0, unroll=2)
    vec_ref[0] += vec_ref[1]
    for i in range(n):
        vx[i] = entry(vec_ref.at[0], 1, 0, i)
    vector_copy = partner_copy(vx, vx_in, 1)
    vector_copy.start()

    def finish(matrix, vector, old_ref, new_ref):
        for i, x in enumerate(solve_rows(matrix, vector)):
            for u in range(units):
                new_ref[u, i : i + 1, :] = old_ref[u, i : i + 1, :] + x[u : u + 1, :ccds]

    finish([[entry(mat_ref, 3, d, n + i) for i in range(n)] for d in range(3)],
           [entry(vec_ref.at[0], 1, 0, n + i) for i in range(n)], field_ref, new_field_ref)
    await_sent(pack, send_sem.at[0])
    await_sent(ans, send_sem.at[1])
    matrix_copy.wait()
    vector_copy.wait()
    finish([[mx[d * n + i] + mx_in[d * n + i] for i in range(n)] for d in range(3)],
           [vx[i] + vx_in[i] for i in range(n)], shared_ref, new_shared_ref)


def hand_on(*refs):
    copies = [pltpu.make_async_copy(refs[i], refs[3 + i], refs[6].at[i]) for i in range(3)]
    for copy in copies:
        copy.start()
    for copy in copies:
        copy.wait()


def per_device(n_tm, observed, weights, features, source_ids, ccd_ids, unit_ids, counts, shared_cal, field_cal):
    slots = observed.shape[1]
    devices = counts.shape[1]
    rows = slots // LANES
    block = rows // devices
    units, n, ccds = shared_cal.shape
    obs, wts, src, ccd, unit = (
        x.reshape(rows, LANES) for x in (observed, weights, source_ids, ccd_ids, unit_ids))
    high = SRC_DEV // LANES
    vm = lambda *shape: pltpu.VMEM(shape, F32)
    vi = lambda *shape: pltpu.VMEM(shape, jnp.int32)
    blocks = lambda kinds: vm(devices, kinds, block, LANES)
    chunks = block * devices // (SUB * CHUNK)
    mean, new_shared, new_field = pl.pallas_call(
        functools.partial(whole_kernel, n_tm, block),
        out_shape=[pltpu.VMEM((high, LANES), F32), pltpu.VMEM((units, n, ccds), F32), pltpu.VMEM((units, n, ccds), F32)],
        in_specs=[pl.BlockSpec(memory_space=pl.ANY)] * 9,
        out_specs=[pl.BlockSpec(memory_space=pltpu.VMEM)] * 3,
        scratch_shapes=[
            vm(rows, LANES), vm(rows, LANES), vi(rows, LANES), vi(rows, LANES), vi(rows, LANES),
            vm(2 * n, slots), pltpu.SMEM((1, devices), jnp.int32), vm(units, n, ccds), vm(units, n, ccds),
            vm(units, 2 * n, LANES), vm(rows, LANES), vm(rows, LANES),
            blocks(3), blocks(3), blocks(1), blocks(1),
            vm(units * 3 * 2 * SUB, CCD_PAD), vm(2, units * 2 * SUB, CCD_PAD), vm(2, 4 * high, LANES),
            vm(3 * n, units, CCD_PAD), vm(3 * n, units, CCD_PAD), vm(n, units, CCD_PAD), vm(n, units, CCD_PAD),
            pltpu.SemaphoreType.DMA((9,)), pltpu.SemaphoreType.DMA((4,)), pltpu.SemaphoreType.DMA((2,)),
            pltpu.SemaphoreType.DMA((2, chunks)),
        ],
        compiler_params=pltpu.CompilerParams(
            collective_id=0, has_side_effects=True, vmem_limit_bytes=56 * 1024 * 1024),
    )(obs, wts, src, ccd, unit, features[0], counts, shared_cal, field_cal[0])
    mean, new_shared, new_field = pl.pallas_call(
        hand_on,
        out_shape=[jax.ShapeDtypeStruct(x.shape, F32) for x in (mean, new_shared, new_field)],
        in_specs=[pl.BlockSpec(memory_space=pl.ANY)] * 3,
        out_specs=[pl.BlockSpec(memory_space=pl.ANY)] * 3,
        scratch_shapes=[pltpu.SemaphoreType.DMA((3,))],
    )(*(pltpu.with_memory_space_constraint(x, pltpu.VMEM) for x in (mean, new_shared, new_field)))
    return mean.reshape(SRC_DEV), new_shared[None], new_field[None]


def solution(mesh):
    in_specs = (
        P("field", "tm"),
        P("field", "tm"),
        P("field", None, "tm"),
        P("field", "tm"),
        P("field", "tm"),
        P("field", "tm"),
        P("field", "tm"),
        P("tm", None, None),
        P("field", "tm", None, None),
    )
    out_specs = (P(("field", "tm")), P("field", "tm", None, None), P("field", "tm", None, None))
    return jax.shard_map(
        functools.partial(per_device, mesh.shape["tm"]), mesh=mesh, in_specs=in_specs, out_specs=out_specs, check_vma=False
    )
```

```python
import functools

import jax
import jax.numpy as jnp
from jax import lax
from jax.experimental import pallas as pl
from jax.experimental.pallas import tpu as pltpu
from jax.sharding import PartitionSpec as P

SRC_DEV = 8192
RIDGE = 1.0
UNROLL = 8
CHUNK = 2
CHUNK_UNROLL = 8
SPAN = 4
WIDE = 2
LANES = 128
SUB = 8
F32 = jnp.float32
BF16 = jnp.bfloat16
CCD_PAD = 64


def split_pair(x):
    high = x.astype(BF16).astype(F32)
    return jnp.concatenate([x, x - high], axis=0).astype(BF16)


def row_of(x, j, rows):
    return jnp.broadcast_to(x[j : j + 1, :], (rows, x.shape[1]))


def bf16_rows(count):
    return lax.broadcasted_iota(jnp.int32, (count, LANES), 0).astype(F32).astype(BF16)


def wide_row(row, count):
    one = jnp.broadcast_to(row.astype(F32), (2 * SUB, LANES)).astype(BF16)
    return jnp.concatenate([one] * (count // (2 * SUB)), axis=0)


def hot_rows(index_row, rows):
    hit = rows == wide_row(index_row, rows.shape[0])
    return jnp.where(hit, jnp.ones_like(rows), jnp.zeros_like(rows))


def pick(table, index):
    return jnp.take_along_axis(table, index, axis=1, mode="promise_in_bounds")


def nt_dot(left, right):
    return lax.dot_general(
        left, right, (((1,), (1,)), ((), ())), preferred_element_type=F32
    )


def build_tables(shared_ref, field_ref, tab_ref):
    units, n_shared, ccds = shared_ref.shape
    tab_ref[...] = jnp.zeros_like(tab_ref)
    for u in range(units):
        tab_ref[u, 0:n_shared, 0:ccds] = shared_ref[u]
        tab_ref[u, n_shared : 2 * n_shared, 0:ccds] = field_ref[u]


def used_weights(g, wts, cnt_ref, rows_per_block):
    sub = lax.broadcasted_iota(jnp.int32, (SUB, LANES), 0)
    lane = lax.broadcasted_iota(jnp.int32, (SUB, LANES), 1)
    position = (sub % rows_per_block) * LANES + lane
    per_group = SUB // rows_per_block
    limit = jnp.full((SUB, LANES), cnt_ref[0, g * per_group], jnp.int32)
    for b in range(1, per_group):
        limit = jnp.where(sub >= b * rows_per_block, cnt_ref[0, g * per_group + b], limit)
    return jnp.where(position < limit, wts, 0.0)


def feat_rows(feat_ref, row):
    return feat_ref[:, pl.ds(pl.multiple_of(row * LANES, LANES), LANES)]


def calibrate_rows(g, obs, ccd, unit, feat_ref, tables):
    index = ccd + (unit & 1) * CCD_PAD
    corrections = []
    for j in range(SUB):
        index_b = row_of(index, j, SUB)
        unit_b = row_of(unit, j, SUB)
        picked = jnp.where(unit_b < 2, pick(tables[0], index_b), pick(tables[1], index_b))
        corrections.append(jnp.sum(feat_rows(feat_ref, g * SUB + j) * picked, axis=0, keepdims=True))
    return obs - jnp.concatenate(corrections, axis=0)


def masked_units(pairs, unit_row, units):
    unit_b = jnp.broadcast_to(unit_row.astype(F32), (2 * SUB, LANES)).astype(BF16)
    zero = jnp.zeros((2 * SUB, LANES), BF16)
    out = []
    for u in range(units):
        own = unit_b == jnp.asarray(u, BF16)
        out += [jnp.where(own, pair, zero) for pair in pairs]
    return jnp.concatenate(out, axis=0)


def matrix_rows(g, weight_used, ccd, unit, feat_ref, units, ccd_rows):
    sub = lax.broadcasted_iota(jnp.int32, (SUB, LANES), 0) % 4
    left, hot = [], []
    for j in range(SUB):
        feats = feat_rows(feat_ref, g * SUB + j)
        weighted = row_of(weight_used, j, SUB) * feats
        next_one = jnp.where(sub == 3, pltpu.roll(feats, 3, 0), pltpu.roll(feats, 7, 0))
        next_two = jnp.where(sub >= 2, pltpu.roll(feats, 2, 0), pltpu.roll(feats, 6, 0))
        pairs = [split_pair(weighted * other) for other in (feats, next_one, next_two)]
        left.append(masked_units(pairs, unit[j : j + 1, :], units))
        hot.append(hot_rows(ccd[j : j + 1, :], ccd_rows))
    return nt_dot(jnp.concatenate(left, axis=1), jnp.concatenate(hot, axis=1))


def vector_rows(g, scaled, ccd, unit, feat_ref, units, ccd_rows):
    left, hot = [], []
    for j in range(SUB):
        feats = feat_rows(feat_ref, g * SUB + j)
        left.append(masked_units([split_pair(row_of(scaled, j, SUB) * feats)], unit[j : j + 1, :], units))
        hot.append(hot_rows(ccd[j : j + 1, :], ccd_rows))
    return nt_dot(jnp.concatenate(left, axis=1), jnp.concatenate(hot, axis=1))


def source_rows(ids, weights, values, high_rows, low_rows):
    high, low = ids >> 7, ids & (LANES - 1)
    pieces = []
    for x in (weights, values):
        top = x.astype(BF16).astype(F32)
        pieces += [top, x - top]
    zero = jnp.zeros_like(high_rows)
    count = high_rows.shape[0]
    left, hot = [], []
    for j in range(SUB):
        hot.append(hot_rows(low[j : j + 1, :], low_rows))
        hit = high_rows == wide_row(high[j : j + 1, :], count)
        left.append(jnp.concatenate(
            [jnp.where(hit, wide_row(x[j : j + 1, :], count), zero) for x in pieces], axis=0))
    return nt_dot(jnp.concatenate(left, axis=1), jnp.concatenate(hot, axis=1))


def read_rows(mean_ref, ids):
    high, low = ids >> 7, ids & (LANES - 1)
    out = jnp.zeros((SUB, LANES), F32)
    for h in range(SRC_DEV // LANES):
        row = jnp.broadcast_to(mean_ref[h : h + 1, :], (SUB, LANES))
        out = jnp.where(high == h, pick(row, low), out)
    return out


def factor_rows(matrix):
    n = len(matrix[0])
    a = [[None] * n for _ in range(n)]
    for i in range(n):
        a[i][i] = matrix[0][i] + RIDGE
        k = (i + 1) % n
        a[i][k] = a[k][i] = matrix[1][i]
    for i in range(n // 2):
        a[i][i + 2] = a[i + 2][i] = matrix[2][i]
    for p in range(n):
        for i in range(p + 1, n):
            factor = a[i][p] / a[p][p]
            for j in range(p + 1, n):
                a[i][j] = a[i][j] - factor * a[p][j]
            a[i][p] = factor
    for p in range(n):
        a[p][p] = 1.0 / a[p][p]
    return a


def solve_rows(a, vector):
    n = len(vector)
    b = list(vector)
    for p in range(n):
        for i in range(p + 1, n):
            b[i] = b[i] - a[i][p] * b[p]
    x = [None] * n
    for i in reversed(range(n)):
        running = b[i]
        for j in range(i + 1, n):
            running = running - a[i][j] * x[j]
        x[i] = running * a[i][i]
    return x


def whole_kernel(
    n_tm, rows_per_block,
    obs_h, wts_h, src_h, ccd_h, unit_h, feat_h, cnt_h, shared_h, field_h,
    mean_ref, new_shared_ref, new_field_ref,
    obs_ref, wts_ref, src_ref, ccd_ref, unit_ref, feat_ref, cnt_ref, shared_ref, field_ref,
    tab_ref, wu_ref, cal_ref, pack, pack_in, ans, ans_in,
    mat_ref, vec_ref, sum_ref, mx, mx_in, vx, vx_in, lu_ref,
    load_sem, send_sem, recv_sem, chunk_sem,
):
    units, n, ccds = shared_ref.shape
    devices = pack.shape[0]
    groups = obs_ref.shape[0] // SUB
    per = SUB // rows_per_block
    chunk = CHUNK * per
    chunks = devices // chunk
    ring = chunks // 2
    field, tm = lax.axis_index("field"), lax.axis_index("tm")
    me = field * n_tm + tm
    my_chunk = me // chunk
    my_part = my_chunk % ring

    def wrap(x, size):
        return jnp.where(x >= size, x - size, x)

    def place(e):
        return jnp.where(e >= n_tm, 1, 0), wrap(e, n_tm)

    barrier = pltpu.get_barrier_semaphore()
    bits = [1 << b for b in range(n_tm.bit_length() - 1)]
    steps = [(1 - 2 * ((tm // bit) % 2)) * bit for bit in bits]
    for k in reversed(range(n_tm)):
        mate = tm + sum(step for bit, step in zip(bits, steps) if k & bit)
        for other in range(2 if k else 1):
            pl.semaphore_signal(
                barrier, inc=1, device_id=(1 - field if other == 0 else field, mate), device_id_type=pl.DeviceIdType.MESH)

    loads = [
        pltpu.make_async_copy(a, b, load_sem.at[i])
        for i, (a, b) in enumerate((
            (wts_h, wts_ref), (src_h, src_ref), (cnt_h, cnt_ref), (shared_h, shared_ref), (field_h, field_ref),
            (obs_h, obs_ref), (ccd_h, ccd_ref), (unit_h, unit_ref), (feat_h, feat_ref)))
    ]
    for load in loads:
        load.start()

    def chunk_late(step):
        return wrap(field + step % 2, 2) * ring + ring - 1 - step // 2

    def chunk_near(step):
        turn, other = step // 2, step % 2
        part = sum((my_part // bit + turn // bit) % 2 * bit for bit in (1 << b for b in range(ring.bit_length() - 1)))
        return wrap(field + other, 2) * ring + part

    def send_chunk(phase, source, landing, c, first=0):
        for i in range(first, chunk):
            e = c * chunk + (me + i) % chunk
            pltpu.make_async_remote_copy(
                src_ref=source.at[e], dst_ref=landing.at[me], send_sem=send_sem.at[phase],
                recv_sem=chunk_sem.at[phase, my_chunk], device_id=place(e), device_id_type=pl.DeviceIdType.MESH).start()
        if first:
            pltpu.make_async_copy(source.at[me], landing.at[me], chunk_sem.at[phase, my_chunk]).start()

    def await_chunk(phase, landing, c):
        part = landing.at[pl.ds(c * chunk, chunk)]
        pltpu.make_async_copy(part, part, chunk_sem.at[phase, c]).wait()

    def await_sent(ref, sem):
        part = ref.at[pl.ds(0, devices - 1)]
        pltpu.make_async_copy(part, part, sem).wait()

    def rows_at(g):
        return pl.ds(pl.multiple_of(g * SUB, SUB), SUB)

    def pair(ref, g, k):
        return jnp.concatenate([ref[g * per + b, k] for b in range(per)], axis=0)

    def ids_in(g):
        return pair(pack_in, g, 0).astype(jnp.int32)

    def put(ref, g, k, x):
        for b in range(per):
            ref[g * per + b, k] = x[b * rows_per_block : (b + 1) * rows_per_block]

    for load in loads:
        load.wait()
    build_tables(shared_ref, field_ref, tab_ref)
    tables = [tab_ref[2 * t] + pltpu.roll(tab_ref[2 * t + 1], CCD_PAD, 1) for t in range(units // 2)]

    def calibrate(g, carry):
        at = rows_at(g)
        wu = used_weights(g, wts_ref[at, :], cnt_ref, rows_per_block)
        cal = calibrate_rows(g, obs_ref[at, :], ccd_ref[at, :], unit_ref[at, :], feat_ref, tables)
        wu_ref[at, :] = wu
        cal_ref[at, :] = cal
        put(pack, g, 0, src_ref[at, :].astype(F32))
        put(pack, g, 1, wu)
        put(pack, g, 2, wu * cal)
        return carry

    lax.fori_loop(0, groups, calibrate, 0, unroll=UNROLL)
    pl.semaphore_wait(barrier, devices - 1)

    def send_pack(step, carry):
        @pl.when(chunk_late(step) != my_chunk)
        def _():
            send_chunk(0, pack, pack_in, chunk_late(step))

        @pl.when(chunk_late(step) == my_chunk)
        def _():
            send_chunk(0, pack, pack_in, my_chunk, 1)

        return carry

    lax.fori_loop(0, chunks, send_pack, 0, unroll=CHUNK_UNROLL)

    ccd_rows, low_rows = bf16_rows(CCD_PAD), bf16_rows(LANES)
    high_rows = bf16_rows(SRC_DEV // LANES)
    mat_ref[...] = jnp.zeros_like(mat_ref)
    vec_ref[...] = jnp.zeros_like(vec_ref)
    sum_ref[...] = jnp.zeros_like(sum_ref)

    def add_matrix(g, carry):
        at = rows_at(g)
        mat_ref[...] += matrix_rows(g, wu_ref[at, :], ccd_ref[at, :], unit_ref[at, :], feat_ref, units, ccd_rows)
        return carry

    lax.fori_loop(0, groups, add_matrix, 0, unroll=UNROLL)

    def entry(ref, pieces, piece, row):
        out = []
        for u in range(units):
            base = (u * pieces + piece) * 2 * SUB + row
            out.append(ref[base : base + 1, :] + ref[base + SUB : base + SUB + 1, :])
        return jnp.concatenate(out, axis=0)

    def partner_copy(source, landing, phase):
        return pltpu.make_async_remote_copy(
            src_ref=source, dst_ref=landing, send_sem=send_sem.at[2 + phase], recv_sem=recv_sem.at[phase],
            device_id=(1 - field, tm), device_id_type=pl.DeviceIdType.MESH)

    for d in range(3):
        for i in range(n):
            mx[d * n + i] = entry(mat_ref, 3, d, i)
    matrix_copy = partner_copy(mx, mx_in, 0)
    matrix_copy.start()

    def add_sources(step, carry):
        parts = [chunk_near(WIDE * step + k) for k in range(WIDE)]
        for c in parts:
            await_chunk(0, pack_in, c)
        total = [sum_ref[k] for k in range(2)]
        for b in range(WIDE * CHUNK):
            g = parts[b // CHUNK] * CHUNK + b % CHUNK
            total[b % 2] += source_rows(ids_in(g), pair(pack_in, g, 1), pair(pack_in, g, 2), high_rows, low_rows)
        for k in range(2):
            sum_ref[k] = total[k]
        return carry

    lax.fori_loop(0, chunks // WIDE, add_sources, 0, unroll=4)
    count = SRC_DEV // LANES
    sums = sum_ref[0] + sum_ref[1]
    mean_ref[...] = (sums[2 * count : 3 * count] + sums[3 * count :]) / ((sums[:count] + sums[count : 2 * count]) + 1.0)

    def answer_chunk(c):
        for b in range(CHUNK):
            g = c * CHUNK + b
            put(ans, g, 0, read_rows(mean_ref, ids_in(g)))

    def answer(step, carry):
        c = chunk_late(chunks - 1 - step)
        answer_chunk(c)

        @pl.when(c != my_chunk)
        def _():
            send_chunk(1, ans, ans_in, c)

        @pl.when(c == my_chunk)
        def _():
            send_chunk(1, ans, ans_in, my_chunk, 1)

        return carry

    lax.fori_loop(0, chunks, answer, 0, unroll=CHUNK_UNROLL)

    def factor(which, matrix):
        rows = factor_rows(matrix)
        for i in range(n):
            for j in range(n):
                lu_ref[which, i * n + j] = rows[i][j]

    factor(0, [[entry(mat_ref, 3, d, n + i) for i in range(n)] for d in range(3)])
    matrix_copy.wait()
    factor(1, [[mx[d * n + i] + mx_in[d * n + i] for i in range(n)] for d in range(3)])

    def add_vector(step, carry):
        parts = [chunk_near(SPAN * step + k) for k in range(SPAN)]
        for c in parts:
            await_chunk(1, ans_in, c)
        total = [vec_ref[k] for k in range(2)]
        for b in range(SPAN * CHUNK):
            g = parts[b // CHUNK] * CHUNK + b % CHUNK
            at = rows_at(g)
            scaled = wu_ref[at, :] * (cal_ref[at, :] - pair(ans_in, g, 0))
            total[b % 2] += vector_rows(g, scaled, ccd_ref[at, :], unit_ref[at, :], feat_ref, units, ccd_rows)
        for k in range(2):
            vec_ref[k] = total[k]
        return carry

    lax.fori_loop(0, chunks // SPAN, add_vector, 0, unroll=2)
    vec_ref[0] += vec_ref[1]
    for i in range(n):
        vx[i] = entry(vec_ref.at[0], 1, 0, i)
    vector_copy = partner_copy(vx, vx_in, 1)
    vector_copy.start()

    def finish(which, vector, old_ref, new_ref):
        rows = [[lu_ref[which, i * n + j] for j in range(n)] for i in range(n)]
        for i, x in enumerate(solve_rows(rows, vector)):
            for u in range(units):
                new_ref[u, i : i + 1, :] = old_ref[u, i : i + 1, :] + x[u : u + 1, :ccds]

    finish(0, [entry(vec_ref.at[0], 1, 0, n + i) for i in range(n)], field_ref, new_field_ref)
    await_sent(pack, send_sem.at[0])
    await_sent(ans, send_sem.at[1])
    vector_copy.wait()
    finish(1, [vx[i] + vx_in[i] for i in range(n)], shared_ref, new_shared_ref)


def hand_on(*refs):
    copies = [pltpu.make_async_copy(refs[i], refs[3 + i], refs[6].at[i]) for i in range(3)]
    for copy in copies:
        copy.start()
    for copy in copies:
        copy.wait()


def per_device(n_tm, observed, weights, features, source_ids, ccd_ids, unit_ids, counts, shared_cal, field_cal):
    slots = observed.shape[1]
    devices = counts.shape[1]
    rows = slots // LANES
    block = rows // devices
    units, n, ccds = shared_cal.shape
    obs, wts, src, ccd, unit = (
        x.reshape(rows, LANES) for x in (observed, weights, source_ids, ccd_ids, unit_ids))
    high = SRC_DEV // LANES
    vm = lambda *shape: pltpu.VMEM(shape, F32)
    vi = lambda *shape: pltpu.VMEM(shape, jnp.int32)
    blocks = lambda kinds: vm(devices, kinds, block, LANES)
    chunks = block * devices // (SUB * CHUNK)
    mean, new_shared, new_field = pl.pallas_call(
        functools.partial(whole_kernel, n_tm, block),
        out_shape=[pltpu.VMEM((high, LANES), F32), pltpu.VMEM((units, n, ccds), F32), pltpu.VMEM((units, n, ccds), F32)],
        in_specs=[pl.BlockSpec(memory_space=pl.ANY)] * 9,
        out_specs=[pl.BlockSpec(memory_space=pltpu.VMEM)] * 3,
        scratch_shapes=[
            vm(rows, LANES), vm(rows, LANES), vi(rows, LANES), vi(rows, LANES), vi(rows, LANES),
            vm(2 * n, slots), pltpu.SMEM((1, devices), jnp.int32), vm(units, n, ccds), vm(units, n, ccds),
            vm(units, 2 * n, LANES), vm(rows, LANES), vm(rows, LANES),
            blocks(3), blocks(3), blocks(1), blocks(1),
            vm(units * 3 * 2 * SUB, CCD_PAD), vm(2, units * 2 * SUB, CCD_PAD), vm(2, 4 * high, LANES),
            vm(3 * n, units, CCD_PAD), vm(3 * n, units, CCD_PAD), vm(n, units, CCD_PAD), vm(n, units, CCD_PAD),
            vm(2, n * n, units, CCD_PAD),
            pltpu.SemaphoreType.DMA((9,)), pltpu.SemaphoreType.DMA((4,)), pltpu.SemaphoreType.DMA((2,)),
            pltpu.SemaphoreType.DMA((2, chunks)),
        ],
        compiler_params=pltpu.CompilerParams(
            collective_id=0, has_side_effects=True, vmem_limit_bytes=56 * 1024 * 1024),
    )(obs, wts, src, ccd, unit, features[0], counts, shared_cal, field_cal[0])
    mean, new_shared, new_field = pl.pallas_call(
        hand_on,
        out_shape=[jax.ShapeDtypeStruct(x.shape, F32) for x in (mean, new_shared, new_field)],
        in_specs=[pl.BlockSpec(memory_space=pl.ANY)] * 3,
        out_specs=[pl.BlockSpec(memory_space=pl.ANY)] * 3,
        scratch_shapes=[pltpu.SemaphoreType.DMA((3,))],
    )(*(pltpu.with_memory_space_constraint(x, pltpu.VMEM) for x in (mean, new_shared, new_field)))
    return mean.reshape(SRC_DEV), new_shared[None], new_field[None]


def solution(mesh):
    in_specs = (
        P("field", "tm"),
        P("field", "tm"),
        P("field", None, "tm"),
        P("field", "tm"),
        P("field", "tm"),
        P("field", "tm"),
        P("field", "tm"),
        P("tm", None, None),
        P("field", "tm", None, None),
    )
    out_specs = (P(("field", "tm")), P("field", "tm", None, None), P("field", "tm", None, None))
    return jax.shard_map(
        functools.partial(per_device, mesh.shape["tm"]), mesh=mesh, in_specs=in_specs, out_specs=out_specs, check_vma=False
    )
```

```python
import functools

import jax
import jax.numpy as jnp
from jax import lax
from jax.experimental import pallas as pl
from jax.experimental.pallas import tpu as pltpu
from jax.sharding import PartitionSpec as P

SRC_DEV = 8192
RIDGE = 1.0
UNROLL = 8
CHUNK = 2
CHUNK_UNROLL = 8
SPAN = 6
WIDE = 2
LANES = 128
SUB = 8
F32 = jnp.float32
BF16 = jnp.bfloat16
CCD_PAD = 64


def split_pair(x):
    high = x.astype(BF16).astype(F32)
    return jnp.concatenate([x, x - high], axis=0).astype(BF16)


def row_of(x, j, rows):
    return jnp.broadcast_to(x[j : j + 1, :], (rows, x.shape[1]))


def bf16_rows(count):
    return lax.broadcasted_iota(jnp.int32, (count, LANES), 0).astype(F32).astype(BF16)


def wide_row(row, count):
    one = jnp.broadcast_to(row.astype(F32), (2 * SUB, LANES)).astype(BF16)
    return jnp.concatenate([one] * (count // (2 * SUB)), axis=0)


def hot_rows(index_row, rows):
    hit = rows == wide_row(index_row, rows.shape[0])
    return jnp.where(hit, jnp.ones_like(rows), jnp.zeros_like(rows))


def pick(table, index):
    return jnp.take_along_axis(table, index, axis=1, mode="promise_in_bounds")


def nt_dot(left, right):
    return lax.dot_general(
        left, right, (((1,), (1,)), ((), ())), preferred_element_type=F32
    )


def build_tables(shared_ref, field_ref, tab_ref):
    units, n_shared, ccds = shared_ref.shape
    tab_ref[...] = jnp.zeros_like(tab_ref)
    for u in range(units):
        tab_ref[u, 0:n_shared, 0:ccds] = shared_ref[u]
        tab_ref[u, n_shared : 2 * n_shared, 0:ccds] = field_ref[u]


def used_weights(g, wts, cnt_ref, rows_per_block):
    sub = lax.broadcasted_iota(jnp.int32, (SUB, LANES), 0)
    lane = lax.broadcasted_iota(jnp.int32, (SUB, LANES), 1)
    position = (sub % rows_per_block) * LANES + lane
    per_group = SUB // rows_per_block
    limit = jnp.full((SUB, LANES), cnt_ref[0, g * per_group], jnp.int32)
    for b in range(1, per_group):
        limit = jnp.where(sub >= b * rows_per_block, cnt_ref[0, g * per_group + b], limit)
    return jnp.where(position < limit, wts, 0.0)


def feat_rows(feat_ref, row):
    return feat_ref[:, pl.ds(pl.multiple_of(row * LANES, LANES), LANES)]


def calibrate_rows(g, obs, ccd, unit, feat_ref, tables):
    index = ccd + (unit & 1) * CCD_PAD
    corrections = []
    for j in range(SUB):
        index_b = row_of(index, j, SUB)
        unit_b = row_of(unit, j, SUB)
        picked = jnp.where(unit_b < 2, pick(tables[0], index_b), pick(tables[1], index_b))
        corrections.append(jnp.sum(feat_rows(feat_ref, g * SUB + j) * picked, axis=0, keepdims=True))
    return obs - jnp.concatenate(corrections, axis=0)


def masked_units(pairs, unit_row, units):
    unit_b = jnp.broadcast_to(unit_row.astype(F32), (2 * SUB, LANES)).astype(BF16)
    zero = jnp.zeros((2 * SUB, LANES), BF16)
    out = []
    for u in range(units):
        own = unit_b == jnp.asarray(u, BF16)
        out += [jnp.where(own, pair, zero) for pair in pairs]
    return jnp.concatenate(out, axis=0)


def matrix_rows(g, weight_used, ccd, unit, feat_ref, units, ccd_rows):
    sub = lax.broadcasted_iota(jnp.int32, (SUB, LANES), 0) % 4
    left, hot = [], []
    for j in range(SUB):
        feats = feat_rows(feat_ref, g * SUB + j)
        weighted = row_of(weight_used, j, SUB) * feats
        next_one = jnp.where(sub == 3, pltpu.roll(feats, 3, 0), pltpu.roll(feats, 7, 0))
        next_two = jnp.where(sub >= 2, pltpu.roll(feats, 2, 0), pltpu.roll(feats, 6, 0))
        pairs = [split_pair(weighted * other) for other in (feats, next_one, next_two)]
        left.append(masked_units(pairs, unit[j : j + 1, :], units))
        hot.append(hot_rows(ccd[j : j + 1, :], ccd_rows))
    return nt_dot(jnp.concatenate(left, axis=1), jnp.concatenate(hot, axis=1))


def vector_rows(g, scaled, ccd, unit, feat_ref, units, ccd_rows):
    left, hot = [], []
    for j in range(SUB):
        feats = feat_rows(feat_ref, g * SUB + j)
        left.append(masked_units([split_pair(row_of(scaled, j, SUB) * feats)], unit[j : j + 1, :], units))
        hot.append(hot_rows(ccd[j : j + 1, :], ccd_rows))
    return nt_dot(jnp.concatenate(left, axis=1), jnp.concatenate(hot, axis=1))


def source_rows(ids, weights, values, high_rows, low_rows):
    high, low = ids >> 7, ids & (LANES - 1)
    pieces = []
    for x in (weights, values):
        top = x.astype(BF16).astype(F32)
        pieces += [top, x - top]
    zero = jnp.zeros_like(high_rows)
    count = high_rows.shape[0]
    left, hot = [], []
    for j in range(SUB):
        hot.append(hot_rows(low[j : j + 1, :], low_rows))
        hit = high_rows == wide_row(high[j : j + 1, :], count)
        left.append(jnp.concatenate(
            [jnp.where(hit, wide_row(x[j : j + 1, :], count), zero) for x in pieces], axis=0))
    return nt_dot(jnp.concatenate(left, axis=1), jnp.concatenate(hot, axis=1))


def read_rows(mean_ref, ids):
    high, low = ids >> 7, ids & (LANES - 1)
    out = jnp.zeros((SUB, LANES), F32)
    for h in range(SRC_DEV // LANES):
        row = jnp.broadcast_to(mean_ref[h : h + 1, :], (SUB, LANES))
        out = jnp.where(high == h, pick(row, low), out)
    return out


def factor_rows(matrix):
    n = len(matrix[0])
    a = [[None] * n for _ in range(n)]
    for i in range(n):
        a[i][i] = matrix[0][i] + RIDGE
        k = (i + 1) % n
        a[i][k] = a[k][i] = matrix[1][i]
    for i in range(n // 2):
        a[i][i + 2] = a[i + 2][i] = matrix[2][i]
    for p in range(n):
        for i in range(p + 1, n):
            factor = a[i][p] / a[p][p]
            for j in range(p + 1, n):
                a[i][j] = a[i][j] - factor * a[p][j]
            a[i][p] = factor
    for p in range(n):
        a[p][p] = 1.0 / a[p][p]
    return a


def solve_rows(a, vector):
    n = len(vector)
    b = list(vector)
    for p in range(n):
        for i in range(p + 1, n):
            b[i] = b[i] - a[i][p] * b[p]
    x = [None] * n
    for i in reversed(range(n)):
        running = b[i]
        for j in range(i + 1, n):
            running = running - a[i][j] * x[j]
        x[i] = running * a[i][i]
    return x


def whole_kernel(
    n_tm, rows_per_block,
    obs_h, wts_h, src_h, ccd_h, unit_h, feat_h, cnt_h, shared_h, field_h,
    mean_ref, new_shared_ref, new_field_ref,
    obs_ref, wts_ref, src_ref, ccd_ref, unit_ref, feat_ref, cnt_ref, shared_ref, field_ref,
    tab_ref, wu_ref, cal_ref, pack, pack_in, ans, ans_in,
    mat_ref, vec_ref, sum_ref, mx, mx_in, vx, vx_in, lu_ref,
    load_sem, send_sem, recv_sem, chunk_sem,
):
    units, n, ccds = shared_ref.shape
    devices = pack.shape[0]
    groups = obs_ref.shape[0] // SUB
    per = SUB // rows_per_block
    chunk = CHUNK * per
    chunks = devices // chunk
    ring = chunks // 2
    field, tm = lax.axis_index("field"), lax.axis_index("tm")
    me = field * n_tm + tm
    my_chunk = me // chunk
    my_part = my_chunk % ring

    def wrap(x, size):
        return jnp.where(x >= size, x - size, x)

    def place(e):
        return jnp.where(e >= n_tm, 1, 0), wrap(e, n_tm)

    barrier = pltpu.get_barrier_semaphore()
    bits = [1 << b for b in range(n_tm.bit_length() - 1)]
    steps = [(1 - 2 * ((tm // bit) % 2)) * bit for bit in bits]
    for k in reversed(range(n_tm)):
        mate = tm + sum(step for bit, step in zip(bits, steps) if k & bit)
        for other in range(2 if k else 1):
            pl.semaphore_signal(
                barrier, inc=1, device_id=(1 - field if other == 0 else field, mate), device_id_type=pl.DeviceIdType.MESH)

    loads = [
        pltpu.make_async_copy(a, b, load_sem.at[i])
        for i, (a, b) in enumerate((
            (wts_h, wts_ref), (src_h, src_ref), (cnt_h, cnt_ref), (shared_h, shared_ref), (field_h, field_ref),
            (obs_h, obs_ref), (ccd_h, ccd_ref), (unit_h, unit_ref), (feat_h, feat_ref)))
    ]
    for load in loads:
        load.start()

    def chunk_late(step):
        return wrap(field + step % 2, 2) * ring + ring - 1 - step // 2

    def chunk_near(step):
        turn, other = step // 2, step % 2
        part = sum((my_part // bit + turn // bit) % 2 * bit for bit in (1 << b for b in range(ring.bit_length() - 1)))
        return wrap(field + other, 2) * ring + part

    def send_chunk(phase, source, landing, c, first=0):
        for i in range(first, chunk):
            e = c * chunk + (me + i) % chunk
            pltpu.make_async_remote_copy(
                src_ref=source.at[e], dst_ref=landing.at[me], send_sem=send_sem.at[phase],
                recv_sem=chunk_sem.at[phase, my_chunk], device_id=place(e), device_id_type=pl.DeviceIdType.MESH).start()
        if first:
            pltpu.make_async_copy(source.at[me], landing.at[me], chunk_sem.at[phase, my_chunk]).start()

    def send_other(phase, source, landing, e):
        @pl.when(e != me)
        def _():
            pltpu.make_async_remote_copy(
                src_ref=source.at[e], dst_ref=landing.at[me], send_sem=send_sem.at[phase],
                recv_sem=chunk_sem.at[phase, my_chunk], device_id=place(e), device_id_type=pl.DeviceIdType.MESH).start()

        @pl.when(e == me)
        def _():
            pltpu.make_async_copy(source.at[me], landing.at[me], chunk_sem.at[phase, my_chunk]).start()

    def await_chunk(phase, landing, c):
        part = landing.at[pl.ds(c * chunk, chunk)]
        pltpu.make_async_copy(part, part, chunk_sem.at[phase, c]).wait()

    def await_sent(ref, sem):
        part = ref.at[pl.ds(0, devices - 1)]
        pltpu.make_async_copy(part, part, sem).wait()

    def rows_at(g):
        return pl.ds(pl.multiple_of(g * SUB, SUB), SUB)

    def pair(ref, g, k):
        return jnp.concatenate([ref[g * per + b, k] for b in range(per)], axis=0)

    def ids_in(g):
        return pair(pack_in, g, 0).astype(jnp.int32)

    def put(ref, g, k, x):
        for b in range(per):
            ref[g * per + b, k] = x[b * rows_per_block : (b + 1) * rows_per_block]

    for load in loads:
        load.wait()
    build_tables(shared_ref, field_ref, tab_ref)
    tables = [tab_ref[2 * t] + pltpu.roll(tab_ref[2 * t + 1], CCD_PAD, 1) for t in range(units // 2)]

    def calibrate(g, carry):
        at = rows_at(g)
        wu = used_weights(g, wts_ref[at, :], cnt_ref, rows_per_block)
        cal = calibrate_rows(g, obs_ref[at, :], ccd_ref[at, :], unit_ref[at, :], feat_ref, tables)
        wu_ref[at, :] = wu
        cal_ref[at, :] = cal
        put(pack, g, 0, src_ref[at, :].astype(F32))
        put(pack, g, 1, wu)
        put(pack, g, 2, wu * cal)
        return carry

    lax.fori_loop(0, groups, calibrate, 0, unroll=UNROLL)
    pl.semaphore_wait(barrier, devices - 1)

    def send_pack(step, carry):
        part = ring - 1 - step
        for i in reversed(range(chunk)):
            for other in range(2):
                send_other(0, pack, pack_in, (wrap(field + other, 2) * ring + part) * chunk + i)
        return carry

    lax.fori_loop(0, ring, send_pack, 0, unroll=CHUNK_UNROLL // 2)

    ccd_rows, low_rows = bf16_rows(CCD_PAD), bf16_rows(LANES)
    high_rows = bf16_rows(SRC_DEV // LANES)
    mat_ref[...] = jnp.zeros_like(mat_ref)
    vec_ref[...] = jnp.zeros_like(vec_ref)
    sum_ref[...] = jnp.zeros_like(sum_ref)

    def add_matrix(g, carry):
        at = rows_at(g)
        mat_ref[...] += matrix_rows(g, wu_ref[at, :], ccd_ref[at, :], unit_ref[at, :], feat_ref, units, ccd_rows)
        return carry

    lax.fori_loop(0, groups, add_matrix, 0, unroll=UNROLL)

    def entry(ref, pieces, piece, row):
        out = []
        for u in range(units):
            base = (u * pieces + piece) * 2 * SUB + row
            out.append(ref[base : base + 1, :] + ref[base + SUB : base + SUB + 1, :])
        return jnp.concatenate(out, axis=0)

    def partner_copy(source, landing, phase):
        return pltpu.make_async_remote_copy(
            src_ref=source, dst_ref=landing, send_sem=send_sem.at[2 + phase], recv_sem=recv_sem.at[phase],
            device_id=(1 - field, tm), device_id_type=pl.DeviceIdType.MESH)

    for d in range(3):
        for i in range(n):
            mx[d * n + i] = entry(mat_ref, 3, d, i)
    matrix_copy = partner_copy(mx, mx_in, 0)
    matrix_copy.start()

    def add_sources(step, carry):
        parts = [chunk_near(WIDE * step + k) for k in range(WIDE)]
        for c in parts:
            await_chunk(0, pack_in, c)
        total = [sum_ref[k] for k in range(2)]
        for b in range(WIDE * CHUNK):
            g = parts[b // CHUNK] * CHUNK + b % CHUNK
            total[b % 2] += source_rows(ids_in(g), pair(pack_in, g, 1), pair(pack_in, g, 2), high_rows, low_rows)
        for k in range(2):
            sum_ref[k] = total[k]
        return carry

    lax.fori_loop(0, chunks // WIDE, add_sources, 0, unroll=4)
    count = SRC_DEV // LANES
    sums = sum_ref[0] + sum_ref[1]
    mean_ref[...] = (sums[2 * count : 3 * count] + sums[3 * count :]) / ((sums[:count] + sums[count : 2 * count]) + 1.0)

    def answer(part, carry):
        for b in range(CHUNK):
            both = [(wrap(field + other, 2) * ring + part) * CHUNK + b for other in range(2)]
            for g in both:
                put(ans, g, 0, read_rows(mean_ref, ids_in(g)))
            for g in both:
                for k in range(per):
                    send_other(1, ans, ans_in, g * per + k)
        return carry

    lax.fori_loop(0, ring, answer, 0, unroll=CHUNK_UNROLL // 2)

    def factor(which, matrix):
        rows = factor_rows(matrix)
        for i in range(n):
            for j in range(n):
                lu_ref[which, i * n + j] = rows[i][j]

    factor(0, [[entry(mat_ref, 3, d, n + i) for i in range(n)] for d in range(3)])
    matrix_copy.wait()
    factor(1, [[mx[d * n + i] + mx_in[d * n + i] for i in range(n)] for d in range(3)])

    def add_vector(start, span):
        parts = [chunk_near(start + k) for k in range(span)]
        for c in parts:
            await_chunk(1, ans_in, c)
        total = [vec_ref[k] for k in range(2)]
        for b in range(span * CHUNK):
            g = parts[b // CHUNK] * CHUNK + b % CHUNK
            at = rows_at(g)
            scaled = wu_ref[at, :] * (cal_ref[at, :] - pair(ans_in, g, 0))
            total[b % 2] += vector_rows(g, scaled, ccd_ref[at, :], unit_ref[at, :], feat_ref, units, ccd_rows)
        for k in range(2):
            vec_ref[k] = total[k]

    def add_early(step, carry):
        add_vector(step * SPAN, SPAN)
        return carry

    lax.fori_loop(0, (chunks - 2) // SPAN, add_early, 0)
    add_vector(chunks - 2, 2)
    vec_ref[0] += vec_ref[1]
    for i in range(n):
        vx[i] = entry(vec_ref.at[0], 1, 0, i)
    vector_copy = partner_copy(vx, vx_in, 1)
    vector_copy.start()

    def finish(which, vector, old_ref, new_ref):
        rows = [[lu_ref[which, i * n + j] for j in range(n)] for i in range(n)]
        for i, x in enumerate(solve_rows(rows, vector)):
            for u in range(units):
                new_ref[u, i : i + 1, :] = old_ref[u, i : i + 1, :] + x[u : u + 1, :ccds]

    finish(0, [entry(vec_ref.at[0], 1, 0, n + i) for i in range(n)], field_ref, new_field_ref)
    await_sent(pack, send_sem.at[0])
    await_sent(ans, send_sem.at[1])
    vector_copy.wait()
    finish(1, [vx[i] + vx_in[i] for i in range(n)], shared_ref, new_shared_ref)


def hand_on(*refs):
    copies = [pltpu.make_async_copy(refs[i], refs[3 + i], refs[6].at[i]) for i in range(3)]
    for copy in copies:
        copy.start()
    for copy in copies:
        copy.wait()


def per_device(n_tm, observed, weights, features, source_ids, ccd_ids, unit_ids, counts, shared_cal, field_cal):
    slots = observed.shape[1]
    devices = counts.shape[1]
    rows = slots // LANES
    block = rows // devices
    units, n, ccds = shared_cal.shape
    obs, wts, src, ccd, unit = (
        x.reshape(rows, LANES) for x in (observed, weights, source_ids, ccd_ids, unit_ids))
    high = SRC_DEV // LANES
    vm = lambda *shape: pltpu.VMEM(shape, F32)
    vi = lambda *shape: pltpu.VMEM(shape, jnp.int32)
    blocks = lambda kinds: vm(devices, kinds, block, LANES)
    chunks = block * devices // (SUB * CHUNK)
    mean, new_shared, new_field = pl.pallas_call(
        functools.partial(whole_kernel, n_tm, block),
        out_shape=[pltpu.VMEM((high, LANES), F32), pltpu.VMEM((units, n, ccds), F32), pltpu.VMEM((units, n, ccds), F32)],
        in_specs=[pl.BlockSpec(memory_space=pl.ANY)] * 9,
        out_specs=[pl.BlockSpec(memory_space=pltpu.VMEM)] * 3,
        scratch_shapes=[
            vm(rows, LANES), vm(rows, LANES), vi(rows, LANES), vi(rows, LANES), vi(rows, LANES),
            vm(2 * n, slots), pltpu.SMEM((1, devices), jnp.int32), vm(units, n, ccds), vm(units, n, ccds),
            vm(units, 2 * n, LANES), vm(rows, LANES), vm(rows, LANES),
            blocks(3), blocks(3), blocks(1), blocks(1),
            vm(units * 3 * 2 * SUB, CCD_PAD), vm(2, units * 2 * SUB, CCD_PAD), vm(2, 4 * high, LANES),
            vm(3 * n, units, CCD_PAD), vm(3 * n, units, CCD_PAD), vm(n, units, CCD_PAD), vm(n, units, CCD_PAD),
            vm(2, n * n, units, CCD_PAD),
            pltpu.SemaphoreType.DMA((9,)), pltpu.SemaphoreType.DMA((4,)), pltpu.SemaphoreType.DMA((2,)),
            pltpu.SemaphoreType.DMA((2, chunks)),
        ],
        compiler_params=pltpu.CompilerParams(
            collective_id=0, has_side_effects=True, vmem_limit_bytes=56 * 1024 * 1024),
    )(obs, wts, src, ccd, unit, features[0], counts, shared_cal, field_cal[0])
    mean, new_shared, new_field = pl.pallas_call(
        hand_on,
        out_shape=[jax.ShapeDtypeStruct(x.shape, F32) for x in (mean, new_shared, new_field)],
        in_specs=[pl.BlockSpec(memory_space=pl.ANY)] * 3,
        out_specs=[pl.BlockSpec(memory_space=pl.ANY)] * 3,
        scratch_shapes=[pltpu.SemaphoreType.DMA((3,))],
    )(*(pltpu.with_memory_space_constraint(x, pltpu.VMEM) for x in (mean, new_shared, new_field)))
    return mean.reshape(SRC_DEV), new_shared[None], new_field[None]


def solution(mesh):
    in_specs = (
        P("field", "tm"),
        P("field", "tm"),
        P("field", None, "tm"),
        P("field", "tm"),
        P("field", "tm"),
        P("field", "tm"),
        P("field", "tm"),
        P("tm", None, None),
        P("field", "tm", None, None),
    )
    out_specs = (P(("field", "tm")), P("field", "tm", None, None), P("field", "tm", None, None))
    return jax.shard_map(
        functools.partial(per_device, mesh.shape["tm"]), mesh=mesh, in_specs=in_specs, out_specs=out_specs, check_vma=False
    )
```

```python
import functools

import jax
import jax.numpy as jnp
from jax import lax
from jax.experimental import pallas as pl
from jax.experimental.pallas import tpu as pltpu
from jax.sharding import PartitionSpec as P

SRC_DEV = 8192
RIDGE = 1.0
UNROLL = 8
CHUNK = 2
CHUNK_UNROLL = 8
SPAN = 6
WIDE = 2
LANES = 128
SUB = 8
F32 = jnp.float32
BF16 = jnp.bfloat16
CCD_PAD = 64


def split_pair(x):
    high = x.astype(BF16).astype(F32)
    return jnp.concatenate([x, x - high], axis=0).astype(BF16)


def row_of(x, j, rows):
    return jnp.broadcast_to(x[j : j + 1, :], (rows, x.shape[1]))


def bf16_rows(count):
    return lax.broadcasted_iota(jnp.int32, (count, LANES), 0).astype(F32).astype(BF16)


def wide_row(row, count):
    one = jnp.broadcast_to(row.astype(F32), (2 * SUB, LANES)).astype(BF16)
    return jnp.concatenate([one] * (count // (2 * SUB)), axis=0)


def hot_rows(index_row, rows):
    hit = rows == wide_row(index_row, rows.shape[0])
    return jnp.where(hit, jnp.ones_like(rows), jnp.zeros_like(rows))


def pick(table, index):
    return jnp.take_along_axis(table, index, axis=1, mode="promise_in_bounds")


def nt_dot(left, right):
    return lax.dot_general(
        left, right, (((1,), (1,)), ((), ())), preferred_element_type=F32
    )


def build_tables(shared_ref, field_ref, tab_ref):
    units, n_shared, ccds = shared_ref.shape
    tab_ref[...] = jnp.zeros_like(tab_ref)
    for u in range(units):
        tab_ref[u, 0:n_shared, 0:ccds] = shared_ref[u]
        tab_ref[u, n_shared : 2 * n_shared, 0:ccds] = field_ref[u]


def used_weights(g, wts, cnt_ref, rows_per_block):
    sub = lax.broadcasted_iota(jnp.int32, (SUB, LANES), 0)
    lane = lax.broadcasted_iota(jnp.int32, (SUB, LANES), 1)
    position = (sub % rows_per_block) * LANES + lane
    per_group = SUB // rows_per_block
    limit = jnp.full((SUB, LANES), cnt_ref[0, g * per_group], jnp.int32)
    for b in range(1, per_group):
        limit = jnp.where(sub >= b * rows_per_block, cnt_ref[0, g * per_group + b], limit)
    return jnp.where(position < limit, wts, 0.0)


def feat_rows(feat_ref, row):
    return feat_ref[:, pl.ds(pl.multiple_of(row * LANES, LANES), LANES)]


def calibrate_rows(g, obs, ccd, unit, feat_ref, tables):
    index = ccd + (unit & 1) * CCD_PAD
    corrections = []
    for j in range(SUB):
        index_b = row_of(index, j, SUB)
        unit_b = row_of(unit, j, SUB)
        picked = jnp.where(unit_b < 2, pick(tables[0], index_b), pick(tables[1], index_b))
        corrections.append(jnp.sum(feat_rows(feat_ref, g * SUB + j) * picked, axis=0, keepdims=True))
    return obs - jnp.concatenate(corrections, axis=0)


def masked_units(pairs, unit_row, units):
    unit_b = jnp.broadcast_to(unit_row.astype(F32), (2 * SUB, LANES)).astype(BF16)
    zero = jnp.zeros((2 * SUB, LANES), BF16)
    out = []
    for u in range(units):
        own = unit_b == jnp.asarray(u, BF16)
        out += [jnp.where(own, pair, zero) for pair in pairs]
    return jnp.concatenate(out, axis=0)


def matrix_rows(g, weight_used, ccd, unit, feat_ref, units, ccd_rows):
    sub = lax.broadcasted_iota(jnp.int32, (SUB, LANES), 0) % 4
    left, hot = [], []
    for j in range(SUB):
        feats = feat_rows(feat_ref, g * SUB + j)
        weighted = row_of(weight_used, j, SUB) * feats
        next_one = jnp.where(sub == 3, pltpu.roll(feats, 3, 0), pltpu.roll(feats, 7, 0))
        next_two = jnp.where(sub >= 2, pltpu.roll(feats, 2, 0), pltpu.roll(feats, 6, 0))
        pairs = [split_pair(weighted * other) for other in (feats, next_one, next_two)]
        left.append(masked_units(pairs, unit[j : j + 1, :], units))
        hot.append(hot_rows(ccd[j : j + 1, :], ccd_rows))
    return nt_dot(jnp.concatenate(left, axis=1), jnp.concatenate(hot, axis=1))


def vector_rows(g, scaled, ccd, unit, feat_ref, units, ccd_rows):
    left, hot = [], []
    for j in range(SUB):
        feats = feat_rows(feat_ref, g * SUB + j)
        left.append(masked_units([split_pair(row_of(scaled, j, SUB) * feats)], unit[j : j + 1, :], units))
        hot.append(hot_rows(ccd[j : j + 1, :], ccd_rows))
    return nt_dot(jnp.concatenate(left, axis=1), jnp.concatenate(hot, axis=1))


def source_rows(ids, weights, values, high_rows, low_rows):
    high, low = ids >> 7, ids & (LANES - 1)
    pieces = []
    for x in (weights, values):
        top = x.astype(BF16).astype(F32)
        pieces += [top, x - top]
    zero = jnp.zeros_like(high_rows)
    count = high_rows.shape[0]
    left, hot = [], []
    for j in range(SUB):
        hot.append(hot_rows(low[j : j + 1, :], low_rows))
        hit = high_rows == wide_row(high[j : j + 1, :], count)
        left.append(jnp.concatenate(
            [jnp.where(hit, wide_row(x[j : j + 1, :], count), zero) for x in pieces], axis=0))
    return nt_dot(jnp.concatenate(left, axis=1), jnp.concatenate(hot, axis=1))


def read_rows(mean_ref, ids):
    high, low = ids >> 7, ids & (LANES - 1)
    out = jnp.zeros((SUB, LANES), F32)
    for h in range(SRC_DEV // LANES):
        row = jnp.broadcast_to(mean_ref[h : h + 1, :], (SUB, LANES))
        out = jnp.where(high == h, pick(row, low), out)
    return out


def factor_rows(matrix):
    n = len(matrix[0])
    a = [[None] * n for _ in range(n)]
    for i in range(n):
        a[i][i] = matrix[0][i] + RIDGE
        k = (i + 1) % n
        a[i][k] = a[k][i] = matrix[1][i]
    for i in range(n // 2):
        a[i][i + 2] = a[i + 2][i] = matrix[2][i]
    for p in range(n):
        for i in range(p + 1, n):
            factor = a[i][p] / a[p][p]
            for j in range(p + 1, n):
                a[i][j] = a[i][j] - factor * a[p][j]
            a[i][p] = factor
    for p in range(n):
        a[p][p] = 1.0 / a[p][p]
    return a


def solve_rows(a, vector):
    n = len(vector)
    b = list(vector)
    for p in range(n):
        for i in range(p + 1, n):
            b[i] = b[i] - a[i][p] * b[p]
    x = [None] * n
    for i in reversed(range(n)):
        running = b[i]
        for j in range(i + 1, n):
            running = running - a[i][j] * x[j]
        x[i] = running * a[i][i]
    return x


def whole_kernel(
    n_tm, rows_per_block,
    obs_h, wts_h, src_h, ccd_h, unit_h, feat_h, cnt_h, shared_h, field_h,
    mean_ref, new_shared_ref, new_field_ref,
    obs_ref, wts_ref, src_ref, ccd_ref, unit_ref, feat_ref, cnt_ref, shared_ref, field_ref,
    tab_ref, wu_ref, cal_ref, pack, pack_in, ans, ans_in,
    mat_ref, vec_ref, sum_ref, mx, mx_in, vx, vx_in, lu_ref,
    load_sem, send_sem, recv_sem, chunk_sem,
):
    units, n, ccds = shared_ref.shape
    devices = pack.shape[0]
    groups = obs_ref.shape[0] // SUB
    per = SUB // rows_per_block
    chunk = CHUNK * per
    chunks = devices // chunk
    ring = chunks // 2
    field, tm = lax.axis_index("field"), lax.axis_index("tm")
    me = field * n_tm + tm
    my_chunk = me // chunk
    my_part = my_chunk % ring

    def wrap(x, size):
        return jnp.where(x >= size, x - size, x)

    def place(e):
        return jnp.where(e >= n_tm, 1, 0), wrap(e, n_tm)

    barrier = pltpu.get_barrier_semaphore()
    bits = [1 << b for b in range(n_tm.bit_length() - 1)]
    steps = [(1 - 2 * ((tm // bit) % 2)) * bit for bit in bits]
    for k in reversed(range(n_tm)):
        mate = tm + sum(step for bit, step in zip(bits, steps) if k & bit)
        for other in range(2 if k else 1):
            pl.semaphore_signal(
                barrier, inc=1, device_id=(1 - field if other == 0 else field, mate), device_id_type=pl.DeviceIdType.MESH)

    loads = [
        pltpu.make_async_copy(a, b, load_sem.at[i])
        for i, (a, b) in enumerate((
            (wts_h, wts_ref), (src_h, src_ref), (cnt_h, cnt_ref), (shared_h, shared_ref), (field_h, field_ref),
            (obs_h, obs_ref), (ccd_h, ccd_ref), (unit_h, unit_ref), (feat_h, feat_ref)))
    ]
    for load in loads:
        load.start()

    def chunk_late(step):
        return wrap(field + step % 2, 2) * ring + ring - 1 - step // 2

    def chunk_near(step):
        turn, other = step // 2, step % 2
        part = sum((my_part // bit + turn // bit) % 2 * bit for bit in (1 << b for b in range(ring.bit_length() - 1)))
        return wrap(field + other, 2) * ring + part

    def send(phase, source, landing, e):
        pltpu.make_async_remote_copy(
            src_ref=source.at[e], dst_ref=landing.at[me], send_sem=send_sem.at[phase],
            recv_sem=chunk_sem.at[phase, my_chunk], device_id=place(e), device_id_type=pl.DeviceIdType.MESH).start()

    def send_all(phase, source, landing, part, blocks):
        @pl.when(part != my_part)
        def _():
            for e in blocks:
                send(phase, source, landing, e)

        @pl.when(part == my_part)
        def _():
            for e in blocks:
                @pl.when(e != me)
                def _():
                    send(phase, source, landing, e)

                @pl.when(e == me)
                def _():
                    pltpu.make_async_copy(source.at[me], landing.at[me], chunk_sem.at[phase, my_chunk]).start()

    def await_chunk(phase, landing, c):
        part = landing.at[pl.ds(c * chunk, chunk)]
        pltpu.make_async_copy(part, part, chunk_sem.at[phase, c]).wait()

    def await_sent(ref, sem):
        part = ref.at[pl.ds(0, devices - 1)]
        pltpu.make_async_copy(part, part, sem).wait()

    def rows_at(g):
        return pl.ds(pl.multiple_of(g * SUB, SUB), SUB)

    def pair(ref, g, k):
        return jnp.concatenate([ref[g * per + b, k] for b in range(per)], axis=0)

    def ids_in(g):
        return pair(pack_in, g, 0).astype(jnp.int32)

    def put(ref, g, k, x):
        for b in range(per):
            ref[g * per + b, k] = x[b * rows_per_block : (b + 1) * rows_per_block]

    for load in loads:
        load.wait()
    build_tables(shared_ref, field_ref, tab_ref)
    tables = [tab_ref[2 * t] + pltpu.roll(tab_ref[2 * t + 1], CCD_PAD, 1) for t in range(units // 2)]

    def calibrate(g, carry):
        at = rows_at(g)
        wu = used_weights(g, wts_ref[at, :], cnt_ref, rows_per_block)
        cal = calibrate_rows(g, obs_ref[at, :], ccd_ref[at, :], unit_ref[at, :], feat_ref, tables)
        wu_ref[at, :] = wu
        cal_ref[at, :] = cal
        put(pack, g, 0, src_ref[at, :].astype(F32))
        put(pack, g, 1, wu)
        put(pack, g, 2, wu * cal)
        return carry

    lax.fori_loop(0, groups, calibrate, 0, unroll=UNROLL)
    pl.semaphore_wait(barrier, devices - 1)

    def send_pack(step, carry):
        part = ring - 1 - step
        sides = [(wrap(field + other, 2) * ring + part) * chunk for other in range(2)]
        send_all(0, pack, pack_in, part, [side + i for i in reversed(range(chunk)) for side in sides])
        return carry

    lax.fori_loop(0, ring, send_pack, 0, unroll=CHUNK_UNROLL // 2)

    ccd_rows, low_rows = bf16_rows(CCD_PAD), bf16_rows(LANES)
    high_rows = bf16_rows(SRC_DEV // LANES)
    mat_ref[...] = jnp.zeros_like(mat_ref)
    vec_ref[...] = jnp.zeros_like(vec_ref)
    sum_ref[...] = jnp.zeros_like(sum_ref)

    def add_matrix(g, carry):
        at = rows_at(g)
        mat_ref[...] += matrix_rows(g, wu_ref[at, :], ccd_ref[at, :], unit_ref[at, :], feat_ref, units, ccd_rows)
        return carry

    lax.fori_loop(0, groups, add_matrix, 0, unroll=UNROLL)

    def entry(ref, pieces, piece, row):
        out = []
        for u in range(units):
            base = (u * pieces + piece) * 2 * SUB + row
            out.append(ref[base : base + 1, :] + ref[base + SUB : base + SUB + 1, :])
        return jnp.concatenate(out, axis=0)

    def partner_copy(source, landing, phase):
        return pltpu.make_async_remote_copy(
            src_ref=source, dst_ref=landing, send_sem=send_sem.at[2 + phase], recv_sem=recv_sem.at[phase],
            device_id=(1 - field, tm), device_id_type=pl.DeviceIdType.MESH)

    for d in range(3):
        for i in range(n):
            mx[d * n + i] = entry(mat_ref, 3, d, i)
    matrix_copy = partner_copy(mx, mx_in, 0)
    matrix_copy.start()

    def add_sources(step, carry):
        parts = [chunk_near(WIDE * step + k) for k in range(WIDE)]
        for c in parts:
            await_chunk(0, pack_in, c)
        total = [sum_ref[k] for k in range(2)]
        for b in range(WIDE * CHUNK):
            g = parts[b // CHUNK] * CHUNK + b % CHUNK
            total[b % 2] += source_rows(ids_in(g), pair(pack_in, g, 1), pair(pack_in, g, 2), high_rows, low_rows)
        for k in range(2):
            sum_ref[k] = total[k]
        return carry

    lax.fori_loop(0, chunks // WIDE, add_sources, 0, unroll=4)
    count = SRC_DEV // LANES
    sums = sum_ref[0] + sum_ref[1]
    mean_ref[...] = (sums[2 * count : 3 * count] + sums[3 * count :]) / ((sums[:count] + sums[count : 2 * count]) + 1.0)

    def answer(part, carry):
        for b in range(CHUNK):
            both = [(wrap(field + other, 2) * ring + part) * CHUNK + b for other in range(2)]
            for g in both:
                put(ans, g, 0, read_rows(mean_ref, ids_in(g)))
            send_all(1, ans, ans_in, part, [g * per + k for k in range(per) for g in both])
        return carry

    lax.fori_loop(0, ring, answer, 0, unroll=CHUNK_UNROLL // 2)

    def factor(which, matrix):
        rows = factor_rows(matrix)
        for i in range(n):
            for j in range(n):
                lu_ref[which, i * n + j] = rows[i][j]

    factor(0, [[entry(mat_ref, 3, d, n + i) for i in range(n)] for d in range(3)])
    matrix_copy.wait()
    factor(1, [[mx[d * n + i] + mx_in[d * n + i] for i in range(n)] for d in range(3)])

    def add_vector(start, span):
        parts = [chunk_near(start + k) for k in range(span)]
        for c in parts:
            await_chunk(1, ans_in, c)
        total = [vec_ref[k] for k in range(2)]
        for b in range(span * CHUNK):
            g = parts[b // CHUNK] * CHUNK + b % CHUNK
            at = rows_at(g)
            scaled = wu_ref[at, :] * (cal_ref[at, :] - pair(ans_in, g, 0))
            total[b % 2] += vector_rows(g, scaled, ccd_ref[at, :], unit_ref[at, :], feat_ref, units, ccd_rows)
        for k in range(2):
            vec_ref[k] = total[k]

    def add_early(step, carry):
        add_vector(step * SPAN, SPAN)
        return carry

    lax.fori_loop(0, (chunks - 2) // SPAN, add_early, 0)
    add_vector(chunks - 2, 2)
    vec_ref[0] += vec_ref[1]
    for i in range(n):
        vx[i] = entry(vec_ref.at[0], 1, 0, i)
    vector_copy = partner_copy(vx, vx_in, 1)
    vector_copy.start()

    def finish(which, vector, old_ref, new_ref):
        rows = [[lu_ref[which, i * n + j] for j in range(n)] for i in range(n)]
        for i, x in enumerate(solve_rows(rows, vector)):
            for u in range(units):
                new_ref[u, i : i + 1, :] = old_ref[u, i : i + 1, :] + x[u : u + 1, :ccds]

    finish(0, [entry(vec_ref.at[0], 1, 0, n + i) for i in range(n)], field_ref, new_field_ref)
    await_sent(pack, send_sem.at[0])
    await_sent(ans, send_sem.at[1])
    vector_copy.wait()
    finish(1, [vx[i] + vx_in[i] for i in range(n)], shared_ref, new_shared_ref)


def hand_on(*refs):
    copies = [pltpu.make_async_copy(refs[i], refs[3 + i], refs[6].at[i]) for i in range(3)]
    for copy in copies:
        copy.start()
    for copy in copies:
        copy.wait()


def per_device(n_tm, observed, weights, features, source_ids, ccd_ids, unit_ids, counts, shared_cal, field_cal):
    slots = observed.shape[1]
    devices = counts.shape[1]
    rows = slots // LANES
    block = rows // devices
    units, n, ccds = shared_cal.shape
    obs, wts, src, ccd, unit = (
        x.reshape(rows, LANES) for x in (observed, weights, source_ids, ccd_ids, unit_ids))
    high = SRC_DEV // LANES
    vm = lambda *shape: pltpu.VMEM(shape, F32)
    vi = lambda *shape: pltpu.VMEM(shape, jnp.int32)
    blocks = lambda kinds: vm(devices, kinds, block, LANES)
    chunks = block * devices // (SUB * CHUNK)
    mean, new_shared, new_field = pl.pallas_call(
        functools.partial(whole_kernel, n_tm, block),
        out_shape=[pltpu.VMEM((high, LANES), F32), pltpu.VMEM((units, n, ccds), F32), pltpu.VMEM((units, n, ccds), F32)],
        in_specs=[pl.BlockSpec(memory_space=pl.ANY)] * 9,
        out_specs=[pl.BlockSpec(memory_space=pltpu.VMEM)] * 3,
        scratch_shapes=[
            vm(rows, LANES), vm(rows, LANES), vi(rows, LANES), vi(rows, LANES), vi(rows, LANES),
            vm(2 * n, slots), pltpu.SMEM((1, devices), jnp.int32), vm(units, n, ccds), vm(units, n, ccds),
            vm(units, 2 * n, LANES), vm(rows, LANES), vm(rows, LANES),
            blocks(3), blocks(3), blocks(1), blocks(1),
            vm(units * 3 * 2 * SUB, CCD_PAD), vm(2, units * 2 * SUB, CCD_PAD), vm(2, 4 * high, LANES),
            vm(3 * n, units, CCD_PAD), vm(3 * n, units, CCD_PAD), vm(n, units, CCD_PAD), vm(n, units, CCD_PAD),
            vm(2, n * n, units, CCD_PAD),
            pltpu.SemaphoreType.DMA((9,)), pltpu.SemaphoreType.DMA((4,)), pltpu.SemaphoreType.DMA((2,)),
            pltpu.SemaphoreType.DMA((2, chunks)),
        ],
        compiler_params=pltpu.CompilerParams(
            collective_id=0, has_side_effects=True, vmem_limit_bytes=56 * 1024 * 1024),
    )(obs, wts, src, ccd, unit, features[0], counts, shared_cal, field_cal[0])
    mean, new_shared, new_field = pl.pallas_call(
        hand_on,
        out_shape=[jax.ShapeDtypeStruct(x.shape, F32) for x in (mean, new_shared, new_field)],
        in_specs=[pl.BlockSpec(memory_space=pl.ANY)] * 3,
        out_specs=[pl.BlockSpec(memory_space=pl.ANY)] * 3,
        scratch_shapes=[pltpu.SemaphoreType.DMA((3,))],
    )(*(pltpu.with_memory_space_constraint(x, pltpu.VMEM) for x in (mean, new_shared, new_field)))
    return mean.reshape(SRC_DEV), new_shared[None], new_field[None]


def solution(mesh):
    in_specs = (
        P("field", "tm"),
        P("field", "tm"),
        P("field", None, "tm"),
        P("field", "tm"),
        P("field", "tm"),
        P("field", "tm"),
        P("field", "tm"),
        P("tm", None, None),
        P("field", "tm", None, None),
    )
    out_specs = (P(("field", "tm")), P("field", "tm", None, None), P("field", "tm", None, None))
    return jax.shard_map(
        functools.partial(per_device, mesh.shape["tm"]), mesh=mesh, in_specs=in_specs, out_specs=out_specs, check_vma=False
    )
```

```python
import functools

import jax
import jax.numpy as jnp
from jax import lax
from jax.experimental import pallas as pl
from jax.experimental.pallas import tpu as pltpu
from jax.sharding import PartitionSpec as P

SRC_DEV = 8192
RIDGE = 1.0
UNROLL = 8
CHUNK = 2
CHUNK_UNROLL = 8
SPAN = 6
WIDE = 2
LANES = 128
SUB = 8
F32 = jnp.float32
BF16 = jnp.bfloat16
CCD_PAD = 64


def split_pair(x):
    high = x.astype(BF16).astype(F32)
    return jnp.concatenate([x, x - high], axis=0).astype(BF16)


def row_of(x, j, rows):
    return jnp.broadcast_to(x[j : j + 1, :], (rows, x.shape[1]))


def bf16_rows(count):
    return lax.broadcasted_iota(jnp.int32, (count, LANES), 0).astype(F32).astype(BF16)


def wide_row(row, count):
    one = jnp.broadcast_to(row.astype(F32), (2 * SUB, LANES)).astype(BF16)
    return jnp.concatenate([one] * (count // (2 * SUB)), axis=0)


def hot_rows(index_row, rows):
    hit = rows == wide_row(index_row, rows.shape[0])
    return jnp.where(hit, jnp.ones_like(rows), jnp.zeros_like(rows))


def pick(table, index):
    return jnp.take_along_axis(table, index, axis=1, mode="promise_in_bounds")


def nt_dot(left, right):
    return lax.dot_general(
        left, right, (((1,), (1,)), ((), ())), preferred_element_type=F32
    )


def build_tables(shared_ref, field_ref, tab_ref):
    units, n_shared, ccds = shared_ref.shape
    tab_ref[...] = jnp.zeros_like(tab_ref)
    for u in range(units):
        tab_ref[u, 0:n_shared, 0:ccds] = shared_ref[u]
        tab_ref[u, n_shared : 2 * n_shared, 0:ccds] = field_ref[u]


def used_weights(g, wts, cnt_ref, rows_per_block):
    sub = lax.broadcasted_iota(jnp.int32, (SUB, LANES), 0)
    lane = lax.broadcasted_iota(jnp.int32, (SUB, LANES), 1)
    position = (sub % rows_per_block) * LANES + lane
    per_group = SUB // rows_per_block
    limit = jnp.full((SUB, LANES), cnt_ref[0, g * per_group], jnp.int32)
    for b in range(1, per_group):
        limit = jnp.where(sub >= b * rows_per_block, cnt_ref[0, g * per_group + b], limit)
    return jnp.where(position < limit, wts, 0.0)


def feat_rows(feat_ref, row):
    return feat_ref[:, pl.ds(pl.multiple_of(row * LANES, LANES), LANES)]


def calibrate_rows(g, obs, ccd, unit, feat_ref, tables):
    index = ccd + (unit & 1) * CCD_PAD
    corrections = []
    for j in range(SUB):
        index_b = row_of(index, j, SUB)
        unit_b = row_of(unit, j, SUB)
        picked = jnp.where(unit_b < 2, pick(tables[0], index_b), pick(tables[1], index_b))
        corrections.append(jnp.sum(feat_rows(feat_ref, g * SUB + j) * picked, axis=0, keepdims=True))
    return obs - jnp.concatenate(corrections, axis=0)


def masked_units(pairs, unit_row, units):
    unit_b = jnp.broadcast_to(unit_row.astype(F32), (2 * SUB, LANES)).astype(BF16)
    zero = jnp.zeros((2 * SUB, LANES), BF16)
    out = []
    for u in range(units):
        own = unit_b == jnp.asarray(u, BF16)
        out += [jnp.where(own, pair, zero) for pair in pairs]
    return jnp.concatenate(out, axis=0)


def matrix_rows(g, weight_used, ccd, unit, feat_ref, units, ccd_rows):
    sub = lax.broadcasted_iota(jnp.int32, (SUB, LANES), 0) % 4
    left, hot = [], []
    for j in range(SUB):
        feats = feat_rows(feat_ref, g * SUB + j)
        weighted = row_of(weight_used, j, SUB) * feats
        next_one = jnp.where(sub == 3, pltpu.roll(feats, 3, 0), pltpu.roll(feats, 7, 0))
        next_two = jnp.where(sub >= 2, pltpu.roll(feats, 2, 0), pltpu.roll(feats, 6, 0))
        pairs = [split_pair(weighted * other) for other in (feats, next_one, next_two)]
        left.append(masked_units(pairs, unit[j : j + 1, :], units))
        hot.append(hot_rows(ccd[j : j + 1, :], ccd_rows))
    return nt_dot(jnp.concatenate(left, axis=1), jnp.concatenate(hot, axis=1))


def vector_rows(g, scaled, ccd, unit, feat_ref, units, ccd_rows):
    left, hot = [], []
    for j in range(SUB):
        feats = feat_rows(feat_ref, g * SUB + j)
        left.append(masked_units([split_pair(row_of(scaled, j, SUB) * feats)], unit[j : j + 1, :], units))
        hot.append(hot_rows(ccd[j : j + 1, :], ccd_rows))
    return nt_dot(jnp.concatenate(left, axis=1), jnp.concatenate(hot, axis=1))


def source_rows(ids, weights, values, high_rows, low_rows):
    high, low = ids >> 7, ids & (LANES - 1)
    pieces = []
    for x in (weights, values):
        top = x.astype(BF16).astype(F32)
        pieces += [top, x - top]
    zero = jnp.zeros_like(high_rows)
    count = high_rows.shape[0]
    left, hot = [], []
    for j in range(SUB):
        hot.append(hot_rows(low[j : j + 1, :], low_rows))
        hit = high_rows == wide_row(high[j : j + 1, :], count)
        left.append(jnp.concatenate(
            [jnp.where(hit, wide_row(x[j : j + 1, :], count), zero) for x in pieces], axis=0))
    return nt_dot(jnp.concatenate(left, axis=1), jnp.concatenate(hot, axis=1))


def read_rows(mean_ref, ids):
    high, low = ids >> 7, ids & (LANES - 1)
    out = jnp.zeros((SUB, LANES), F32)
    for h in range(SRC_DEV // LANES):
        row = jnp.broadcast_to(mean_ref[h : h + 1, :], (SUB, LANES))
        out = jnp.where(high == h, pick(row, low), out)
    return out


def factor_rows(matrix):
    n = len(matrix[0])
    a = [[None] * n for _ in range(n)]
    for i in range(n):
        a[i][i] = matrix[0][i] + RIDGE
        k = (i + 1) % n
        a[i][k] = a[k][i] = matrix[1][i]
    for i in range(n // 2):
        a[i][i + 2] = a[i + 2][i] = matrix[2][i]
    for p in range(n):
        for i in range(p + 1, n):
            factor = a[i][p] / a[p][p]
            for j in range(p + 1, n):
                a[i][j] = a[i][j] - factor * a[p][j]
            a[i][p] = factor
    for p in range(n):
        a[p][p] = 1.0 / a[p][p]
    return a


def solve_rows(a, vector):
    n = len(vector)
    b = list(vector)
    for p in range(n):
        for i in range(p + 1, n):
            b[i] = b[i] - a[i][p] * b[p]
    x = [None] * n
    for i in reversed(range(n)):
        running = b[i]
        for j in range(i + 1, n):
            running = running - a[i][j] * x[j]
        x[i] = running * a[i][i]
    return x


def whole_kernel(
    n_tm, rows_per_block,
    obs_h, wts_h, src_h, ccd_h, unit_h, feat_h, cnt_h, shared_h, field_h,
    mean_ref, new_shared_ref, new_field_ref,
    obs_ref, wts_ref, src_ref, ccd_ref, unit_ref, feat_ref, cnt_ref, shared_ref, field_ref,
    tab_ref, wu_ref, cal_ref, pack, pack_in, ans, ans_in,
    mat_ref, vec_ref, sum_ref, mx, mx_in, vx, vx_in, lu_ref,
    load_sem, send_sem, recv_sem, chunk_sem,
):
    units, n, ccds = shared_ref.shape
    devices = pack.shape[0]
    groups = obs_ref.shape[0] // SUB
    per = SUB // rows_per_block
    chunk = CHUNK * per
    chunks = devices // chunk
    ring = chunks // 2
    field, tm = lax.axis_index("field"), lax.axis_index("tm")
    me = field * n_tm + tm
    my_chunk = me // chunk
    my_part = my_chunk % ring

    def wrap(x, size):
        return jnp.where(x >= size, x - size, x)

    def place(e):
        return jnp.where(e >= n_tm, 1, 0), wrap(e, n_tm)

    barrier = pltpu.get_barrier_semaphore()
    bits = [1 << b for b in range(n_tm.bit_length() - 1)]
    steps = [(1 - 2 * ((tm // bit) % 2)) * bit for bit in bits]
    for k in reversed(range(n_tm)):
        mate = tm + sum(step for bit, step in zip(bits, steps) if k & bit)
        for other in range(2 if k else 1):
            pl.semaphore_signal(
                barrier, inc=1, device_id=(1 - field if other == 0 else field, mate), device_id_type=pl.DeviceIdType.MESH)

    loads = [
        pltpu.make_async_copy(a, b, load_sem.at[i])
        for i, (a, b) in enumerate((
            (wts_h, wts_ref), (src_h, src_ref), (cnt_h, cnt_ref), (shared_h, shared_ref), (field_h, field_ref),
            (obs_h, obs_ref), (ccd_h, ccd_ref), (unit_h, unit_ref), (feat_h, feat_ref)))
    ]
    for load in loads:
        load.start()

    def chunk_late(step):
        return wrap(field + step % 2, 2) * ring + ring - 1 - step // 2

    def chunk_near(step):
        turn, other = step // 2, step % 2
        part = sum((my_part // bit + turn // bit) % 2 * bit for bit in (1 << b for b in range(ring.bit_length() - 1)))
        return wrap(field + other, 2) * ring + part

    def send(phase, source, landing, e):
        pltpu.make_async_remote_copy(
            src_ref=source.at[e], dst_ref=landing.at[me], send_sem=send_sem.at[phase],
            recv_sem=chunk_sem.at[phase, my_chunk], device_id=place(e), device_id_type=pl.DeviceIdType.MESH).start()

    def send_all(phase, source, landing, part, blocks):
        @pl.when(part != my_part)
        def _():
            for e in blocks:
                send(phase, source, landing, e)

        @pl.when(part == my_part)
        def _():
            for e in blocks:
                @pl.when(e != me)
                def _():
                    send(phase, source, landing, e)

                @pl.when(e == me)
                def _():
                    pltpu.make_async_copy(source.at[me], landing.at[me], chunk_sem.at[phase, my_chunk]).start()

    def await_chunk(phase, landing, c):
        part = landing.at[pl.ds(c * chunk, chunk)]
        pltpu.make_async_copy(part, part, chunk_sem.at[phase, c]).wait()

    def await_sent(ref, sem):
        part = ref.at[pl.ds(0, devices - 1)]
        pltpu.make_async_copy(part, part, sem).wait()

    def rows_at(g):
        return pl.ds(pl.multiple_of(g * SUB, SUB), SUB)

    def pair(ref, g, k):
        return jnp.concatenate([ref[g * per + b, k] for b in range(per)], axis=0)

    def ids_in(g):
        return pair(pack_in, g, 0).astype(jnp.int32)

    def put(ref, g, k, x):
        for b in range(per):
            ref[g * per + b, k] = x[b * rows_per_block : (b + 1) * rows_per_block]

    for load in loads:
        load.wait()
    build_tables(shared_ref, field_ref, tab_ref)
    tables = [tab_ref[2 * t] + pltpu.roll(tab_ref[2 * t + 1], CCD_PAD, 1) for t in range(units // 2)]

    def calibrate(g, carry):
        at = rows_at(g)
        wu = used_weights(g, wts_ref[at, :], cnt_ref, rows_per_block)
        cal = calibrate_rows(g, obs_ref[at, :], ccd_ref[at, :], unit_ref[at, :], feat_ref, tables)
        wu_ref[at, :] = wu
        cal_ref[at, :] = cal
        put(pack, g, 0, src_ref[at, :].astype(F32))
        put(pack, g, 1, wu)
        put(pack, g, 2, wu * cal)
        return carry

    lax.fori_loop(0, groups, calibrate, 0, unroll=UNROLL)
    pl.semaphore_wait(barrier, devices - 1)

    def send_pack(step, carry):
        part = ring - 1 - step
        sides = [(wrap(field + other, 2) * ring + part) * chunk for other in range(2)]
        send_all(0, pack, pack_in, part, [side + i for i in reversed(range(chunk)) for side in sides])
        return carry

    lax.fori_loop(0, ring, send_pack, 0, unroll=CHUNK_UNROLL // 2)

    ccd_rows, low_rows = bf16_rows(CCD_PAD), bf16_rows(LANES)
    high_rows = bf16_rows(SRC_DEV // LANES)
    mat_ref[...] = jnp.zeros_like(mat_ref)
    vec_ref[...] = jnp.zeros_like(vec_ref)
    sum_ref[...] = jnp.zeros_like(sum_ref)

    def add_matrix(g, carry):
        at = rows_at(g)
        mat_ref[...] += matrix_rows(g, wu_ref[at, :], ccd_ref[at, :], unit_ref[at, :], feat_ref, units, ccd_rows)
        return carry

    lax.fori_loop(0, groups, add_matrix, 0, unroll=UNROLL)

    def entry(ref, pieces, piece, row):
        out = []
        for u in range(units):
            base = (u * pieces + piece) * 2 * SUB + row
            out.append(ref[base : base + 1, :] + ref[base + SUB : base + SUB + 1, :])
        return jnp.concatenate(out, axis=0)

    def partner_copy(source, landing, phase):
        return pltpu.make_async_remote_copy(
            src_ref=source, dst_ref=landing, send_sem=send_sem.at[2 + phase], recv_sem=recv_sem.at[phase],
            device_id=(1 - field, tm), device_id_type=pl.DeviceIdType.MESH)

    for d in range(3):
        for i in range(n):
            mx[d * n + i] = entry(mat_ref, 3, d, i)
    matrix_copy = partner_copy(mx, mx_in, 0)
    matrix_copy.start()

    def add_sources(step, carry):
        parts = [chunk_near(WIDE * step + k) for k in range(WIDE)]
        for c in parts:
            await_chunk(0, pack_in, c)
        total = [sum_ref[k] for k in range(2)]
        for b in range(WIDE * CHUNK):
            g = parts[b // CHUNK] * CHUNK + b % CHUNK
            total[b % 2] += source_rows(ids_in(g), pair(pack_in, g, 1), pair(pack_in, g, 2), high_rows, low_rows)
        for k in range(2):
            sum_ref[k] = total[k]
        return carry

    lax.fori_loop(0, chunks // WIDE, add_sources, 0, unroll=4)
    count = SRC_DEV // LANES
    sums = sum_ref[0] + sum_ref[1]
    mean_ref[...] = (sums[2 * count : 3 * count] + sums[3 * count :]) / ((sums[:count] + sums[count : 2 * count]) + 1.0)

    def answer(part, carry):
        for b in range(CHUNK):
            for other in range(2):
                g = (wrap(field + other, 2) * ring + part) * CHUNK + b
                put(ans, g, 0, read_rows(mean_ref, ids_in(g)))
                send_all(1, ans, ans_in, part, [g * per + k for k in range(per)])
        return carry

    lax.fori_loop(0, ring, answer, 0, unroll=CHUNK_UNROLL // 2)

    def factor(which, matrix):
        rows = factor_rows(matrix)
        for i in range(n):
            for j in range(n):
                lu_ref[which, i * n + j] = rows[i][j]

    factor(0, [[entry(mat_ref, 3, d, n + i) for i in range(n)] for d in range(3)])
    matrix_copy.wait()
    factor(1, [[mx[d * n + i] + mx_in[d * n + i] for i in range(n)] for d in range(3)])

    def add_vector(start, span):
        parts = [chunk_near(start + k) for k in range(span)]
        for c in parts:
            await_chunk(1, ans_in, c)
        total = [vec_ref[k] for k in range(2)]
        for b in range(span * CHUNK):
            g = parts[b // CHUNK] * CHUNK + b % CHUNK
            at = rows_at(g)
            scaled = wu_ref[at, :] * (cal_ref[at, :] - pair(ans_in, g, 0))
            total[b % 2] += vector_rows(g, scaled, ccd_ref[at, :], unit_ref[at, :], feat_ref, units, ccd_rows)
        for k in range(2):
            vec_ref[k] = total[k]

    def add_early(step, carry):
        add_vector(step * SPAN, SPAN)
        return carry

    lax.fori_loop(0, (chunks - 2) // SPAN, add_early, 0)
    add_vector(chunks - 2, 2)
    vec_ref[0] += vec_ref[1]
    for i in range(n):
        vx[i] = entry(vec_ref.at[0], 1, 0, i)
    vector_copy = partner_copy(vx, vx_in, 1)
    vector_copy.start()

    def finish(which, vector, old_ref, new_ref):
        rows = [[lu_ref[which, i * n + j] for j in range(n)] for i in range(n)]
        for i, x in enumerate(solve_rows(rows, vector)):
            for u in range(units):
                new_ref[u, i : i + 1, :] = old_ref[u, i : i + 1, :] + x[u : u + 1, :ccds]

    finish(0, [entry(vec_ref.at[0], 1, 0, n + i) for i in range(n)], field_ref, new_field_ref)
    await_sent(pack, send_sem.at[0])
    await_sent(ans, send_sem.at[1])
    vector_copy.wait()
    finish(1, [vx[i] + vx_in[i] for i in range(n)], shared_ref, new_shared_ref)


def hand_on(*refs):
    copies = [pltpu.make_async_copy(refs[i], refs[3 + i], refs[6].at[i]) for i in range(3)]
    for copy in copies:
        copy.start()
    for copy in copies:
        copy.wait()


def per_device(n_tm, observed, weights, features, source_ids, ccd_ids, unit_ids, counts, shared_cal, field_cal):
    slots = observed.shape[1]
    devices = counts.shape[1]
    rows = slots // LANES
    block = rows // devices
    units, n, ccds = shared_cal.shape
    obs, wts, src, ccd, unit = (
        x.reshape(rows, LANES) for x in (observed, weights, source_ids, ccd_ids, unit_ids))
    high = SRC_DEV // LANES
    vm = lambda *shape: pltpu.VMEM(shape, F32)
    vi = lambda *shape: pltpu.VMEM(shape, jnp.int32)
    blocks = lambda kinds: vm(devices, kinds, block, LANES)
    chunks = block * devices // (SUB * CHUNK)
    mean, new_shared, new_field = pl.pallas_call(
        functools.partial(whole_kernel, n_tm, block),
        out_shape=[pltpu.VMEM((high, LANES), F32), pltpu.VMEM((units, n, ccds), F32), pltpu.VMEM((units, n, ccds), F32)],
        in_specs=[pl.BlockSpec(memory_space=pl.ANY)] * 9,
        out_specs=[pl.BlockSpec(memory_space=pltpu.VMEM)] * 3,
        scratch_shapes=[
            vm(rows, LANES), vm(rows, LANES), vi(rows, LANES), vi(rows, LANES), vi(rows, LANES),
            vm(2 * n, slots), pltpu.SMEM((1, devices), jnp.int32), vm(units, n, ccds), vm(units, n, ccds),
            vm(units, 2 * n, LANES), vm(rows, LANES), vm(rows, LANES),
            blocks(3), blocks(3), blocks(1), blocks(1),
            vm(units * 3 * 2 * SUB, CCD_PAD), vm(2, units * 2 * SUB, CCD_PAD), vm(2, 4 * high, LANES),
            vm(3 * n, units, CCD_PAD), vm(3 * n, units, CCD_PAD), vm(n, units, CCD_PAD), vm(n, units, CCD_PAD),
            vm(2, n * n, units, CCD_PAD),
            pltpu.SemaphoreType.DMA((9,)), pltpu.SemaphoreType.DMA((4,)), pltpu.SemaphoreType.DMA((2,)),
            pltpu.SemaphoreType.DMA((2, chunks)),
        ],
        compiler_params=pltpu.CompilerParams(
            collective_id=0, has_side_effects=True, vmem_limit_bytes=56 * 1024 * 1024),
    )(obs, wts, src, ccd, unit, features[0], counts, shared_cal, field_cal[0])
    mean, new_shared, new_field = pl.pallas_call(
        hand_on,
        out_shape=[jax.ShapeDtypeStruct(x.shape, F32) for x in (mean, new_shared, new_field)],
        in_specs=[pl.BlockSpec(memory_space=pl.ANY)] * 3,
        out_specs=[pl.BlockSpec(memory_space=pl.ANY)] * 3,
        scratch_shapes=[pltpu.SemaphoreType.DMA((3,))],
    )(*(pltpu.with_memory_space_constraint(x, pltpu.VMEM) for x in (mean, new_shared, new_field)))
    return mean.reshape(SRC_DEV), new_shared[None], new_field[None]


def solution(mesh):
    in_specs = (
        P("field", "tm"),
        P("field", "tm"),
        P("field", None, "tm"),
        P("field", "tm"),
        P("field", "tm"),
        P("field", "tm"),
        P("field", "tm"),
        P("tm", None, None),
        P("field", "tm", None, None),
    )
    out_specs = (P(("field", "tm")), P("field", "tm", None, None), P("field", "tm", None, None))
    return jax.shard_map(
        functools.partial(per_device, mesh.shape["tm"]), mesh=mesh, in_specs=in_specs, out_specs=out_specs, check_vma=False
    )
```
